256 devices in a mesh: lat: 4 (over x_lo, core), lon: 64 (over y, z, x_hi).
Axes of the slice: x: 4 (x_hi: 2, x_lo: 2; x = x_hi * 2 + x_lo), y: 4, z: 8, core: 2. Of those that a mesh axis runs over, the one named last changes fastest.
Arguments:
- prognostic: float32 [5, 8, 2880, 1440], P(None, None, 'lon', 'lat'), may hold values from -6 to 6
- filter_rows: int32 [128], replicated, may hold values from 0 to 1439, as said below
- cutoff: int32 [128], replicated, may hold values from 360 to 1439
Outputs:
- advanced: float32 [5, 8, 2880, 1440], P(None, None, 'lon', 'lat')
The draws below stay inside these ranges and needn't reach their ends.
Inputs may be any that keep to these rules, and one draw needn't show every extreme that they name: `filter_rows`: the first 64 entries are distinct rows of the southern band (0 to 359) in rising order, always including row 0; the last 64 are distinct rows of the northern band (1080 to 1439) in rising order, always including row 1439.
All inputs are finite; a program needn't handle non-finite values.
Results may differ from the reference program's by a relative error of at most 0.0001.
Values sent between devices are 32-bit elements; how exact they have to be, the bound alone decides.
No kernel may reach another device: no remote copies, remote signals or barrier semaphores. Data moves between devices by JAX's collectives and lax.ppermute only.
A program may use at most 192 MiB of HBM per device.

```python
import jax
import jax.numpy as jnp

NLON = 2880
NLAT_W = 1440
LEV = 8
FIELDS = 5
SUBSTEPS = 2
FROWS = 64
ROWS_DEV = 360


def draw_filter_rows(key, part):
    south_key = jax.random.fold_in(key, 11)
    north_key = jax.random.fold_in(key, 12)
    southern = jnp.sort(jax.random.permutation(south_key, ROWS_DEV - 1)[:FROWS - 1] + 1)
    northern = jnp.sort(NLAT_W - 2 - jax.random.permutation(north_key, ROWS_DEV - 1)[:FROWS - 1])
    first_row = jnp.zeros((1,), jnp.int32)
    last_row = jnp.full((1,), NLAT_W - 1, jnp.int32)
    return jnp.concatenate([first_row, southern.astype(jnp.int32), northern.astype(jnp.int32), last_row])


def with_ends(drawn, stream_key, low, top_value):
    spot = [jax.random.randint(jax.random.fold_in(stream_key, axis), (), 0, length) for axis, length in enumerate(drawn.shape)]
    longest = drawn.shape.index(max(drawn.shape))
    next_to = spot[:longest] + [(spot[longest] + 1) % drawn.shape[longest]] + spot[longest + 1:]
    return drawn.at[tuple(spot)].set(low).at[tuple(next_to)].set(top_value)


def block_scale(stream_key, dims, cuts, least, high):
    gain, own = 1.0, jax.random.fold_in(stream_key, 6)
    for axis_at, shards_of in cuts:
        draws = jnp.exp(jax.random.uniform(jax.random.fold_in(own, axis_at), (shards_of,), jnp.float32, least / len(cuts), high / len(cuts)))
        gain = gain * jnp.repeat(draws, dims[axis_at] // shards_of).reshape([-1 if axis == axis_at else 1 for axis in range(len(dims))])
    return gain


def centred(key, dims, deviation, limit, cuts=(), kind=jnp.bfloat16):
    array = jax.random.normal(key, dims, jnp.float32) * deviation
    if len(cuts) > 0:
        array = block_scale(key, dims, cuts, -0.22, 0.18) * array
    return jnp.clip(array, min=-limit, max=limit).astype(kind)


def setup_inputs(seed: int = 0) -> dict:
    arg_keys = jax.random.split(jax.random.key(seed), 4)
    return {
        "prognostic": centred(arg_keys[0], (FIELDS, LEV, NLON, NLAT_W), 1.0, 6.0, ((2, 64), (3, 4)), jnp.float32),
        "filter_rows": draw_filter_rows(jax.random.fold_in(arg_keys[3], 71), 0),
        "cutoff": with_ends(jax.random.randint(arg_keys[2], (2 * FROWS,), NLON // 8, NLON // 2), jax.random.fold_in(arg_keys[2], 1), NLON // 8, (NLON // 2) - 1).astype(jnp.int32),
    }


meridional_courant = 0.5
vertical_courant = 0.5
buoyancy_rate = 0.3
polar_courant = 0.5
coriolis_rate = 0.2


def row_angles(first, row_total, length):
    position = (first + jnp.arange(length)).astype(jnp.float32)
    return (position + 0.5) * (jnp.pi / row_total)


def vertical_difference(field):
    padded = jnp.pad(field, ((1, 1), (0, 0), (0, 0)))
    return (padded[2:] - padded[:-2]) * 0.5


def pole_extend(field, sign_flip):
    halfway = field.shape[-2] // 2
    southern = jnp.roll(field[..., :1], -halfway, axis=-2) * sign_flip
    northern = jnp.roll(field[..., -1:], -halfway, axis=-2) * sign_flip
    stacked = jnp.concatenate([southern, field, northern], axis=-1)
    return jnp.concatenate([stacked[..., -1:, :], stacked, stacked[..., :1, :]], axis=-2)


def acoustic_update(state, cosine, sine_lat, polar_cos):
    zonal_wind = state[0]
    north_wind = state[1]
    vertical = state[2]
    pressure = state[3]
    potential = state[4]
    zonal_courant = polar_courant * polar_cos / cosine[1:-1]
    coriolis = coriolis_rate * sine_lat[1:-1]
    pressure_pad = pole_extend(pressure[None], 1.0)[0]
    zonal_gradient = (pressure_pad[:, 2:, 1:-1] - pressure_pad[:, :-2, 1:-1]) * 0.5
    north_gradient = (pressure_pad[:, 1:-1, 2:] - pressure_pad[:, 1:-1, :-2]) * 0.5
    zonal_next = zonal_wind - zonal_courant * zonal_gradient + coriolis * north_wind
    north_next = north_wind - meridional_courant * north_gradient - coriolis * zonal_wind
    vertical_next = vertical - vertical_courant * vertical_difference(pressure) + buoyancy_rate * potential
    winds = pole_extend(jnp.stack([zonal_next, north_next]), -1.0)
    zonal_change = (winds[0, :, 2:, 1:-1] - winds[0, :, :-2, 1:-1]) * 0.5
    north_flux = winds[1] * cosine
    north_change = (north_flux[:, 1:-1, 2:] - north_flux[:, 1:-1, :-2]) * 0.5 / cosine[1:-1]
    divergence = zonal_courant * zonal_change + meridional_courant * north_change + vertical_courant * vertical_difference(vertical_next)
    pressure_next = pressure - divergence
    potential_next = potential - buoyancy_rate * vertical_next
    return jnp.stack([zonal_next, north_next, vertical_next, pressure_next, potential_next])


def polar_filter(state, filter_rows, cutoff):
    row_data = state[:, :, :, filter_rows]
    spectrum = jnp.fft.rfft(row_data, axis=-2)
    wavenumber = jnp.arange(NLON // 2 + 1).astype(jnp.int32)
    keep_mask = wavenumber[:, None] <= cutoff[None, :]
    spectrum = jnp.where(keep_mask, spectrum, jnp.zeros_like(spectrum))
    filtered = jnp.fft.irfft(spectrum, n=NLON, axis=-2).astype(state.dtype)
    return state.at[:, :, :, filter_rows].set(filtered)


def reference(prognostic, filter_rows, cutoff):
    phase_angle = row_angles(-1, NLAT_W, NLAT_W + 2)
    cosine = jnp.abs(jnp.sin(phase_angle))
    sine_lat = -jnp.cos(phase_angle)
    polar_cos = jnp.abs(jnp.sin(row_angles(0, NLAT_W, 1)))[0]
    state = prognostic
    for substep_index in range(SUBSTEPS):
        state = acoustic_update(state, cosine, sine_lat, polar_cos)
        state = polar_filter(state, filter_rows, cutoff)
    return state
```

```python
import jax
import jax.numpy as jnp
import ml_dtypes
import numpy as np
from jax import lax
from jax.experimental import pallas as pl
from jax.experimental.pallas import tpu as pltpu
from jax.sharding import PartitionSpec as P

NLON, NLAT, LEV = 2880, 1440, 8
SEG, BAND, FROWS = 45, 360, 64
F32, BF16, I32 = jnp.float32, jnp.bfloat16, jnp.int32
NN = (((1,), (0,)), ((), ()))
NT = (((1,), (1,)), ((), ()))
TN = (((0,), (0,)), ((), ()))

SLOT_BASE = (0, 12, 22, 30, 38, 46, 54)
SLOT_COUNT = (12, 10, 8, 8, 8, 8, 8)
SLOT_FIRST = (-2, -1, 0, 0, 0, 0, 0)
PAIRS = 17


def slot_tables():
    rho = np.full(64, -100, np.int32)
    kind = np.full(64, -1, np.int32)
    for f, (base, count, first) in enumerate(zip(SLOT_BASE, SLOT_COUNT, SLOT_FIRST)):
        rho[base : base + count] = first + np.arange(count)
        kind[base : base + count] = f
    return rho, kind


def split_np(m):
    high = m.astype(ml_dtypes.bfloat16)
    low = (m - high.astype(np.float64)).astype(ml_dtypes.bfloat16)
    return high, low


def triple(m):
    high, low = split_np(m)
    return np.concatenate([high, low, high], axis=-1)


def fourier_constants():
    s = np.arange(64)
    k1 = np.arange(33)
    ang = 2 * np.pi * (np.outer(k1, s) % 64) / 64
    fwd = np.zeros((80, 64))
    fwd[:33], fwd[40:73] = np.cos(ang), -np.sin(ang)
    inv = np.zeros((2, 64, 2, 24))
    sig = np.zeros((PAIRS, 96, 128))
    mf = np.zeros((2 * PAIRS, 192, 48))
    mi = np.zeros((PAIRS, 192, 96))
    i, k2 = np.arange(SEG), np.arange(SEG)
    for q in range(33):
        half, pair = divmod(q, PAIRS)
        inv[half, :, 0, pair] = np.cos(ang[q])
        inv[half, :, 1, pair] = -np.sin(ang[q])
        k = q + 64 * k2
        w = 2 * np.pi * (np.outer(k, i) % NLON) / NLON
        full = np.zeros((2, 48, 2, 48))
        full[0, :SEG, 0, :SEG], full[0, :SEG, 1, :SEG] = np.cos(w), np.sin(w)
        full[1, :SEG, 0, :SEG], full[1, :SEG, 1, :SEG] = -np.sin(w), np.cos(w)
        for h in range(2):
            mf[q, 96 * h : 96 * h + 96] = full[:, :, :, 24 * h : 24 * h + 24].reshape(96, 48)
        scale = (1.0 if q in (0, 32) else 2.0) / NLON
        mi[pair, 96 * half : 96 * half + 96] = full.reshape(96, 96).T * scale
        sn = np.sin(2 * np.pi * k / NLON)
        sig[pair, :SEG, 64 * half : 64 * half + 64] = -sn[:, None]
        sig[pair, 48 : 48 + SEG, 64 * half : 64 * half + 64] = sn[:, None]
    mih, mil = split_np(mi)
    return (
        triple(fwd),
        triple(mf),
        np.concatenate([mih, mil], axis=-1),
        mih,
        triple(inv.reshape(128, 48)),
        sig.astype(np.float32),
    )


def dot(a, b, dims=NN):
    return lax.dot_general(a, b, dims, preferred_element_type=F32)


def split(x):
    high = x.astype(BF16)
    return high, (x - high.astype(F32)).astype(BF16)


def iota(shape, axis):
    return lax.broadcasted_iota(I32, shape, axis)


def edge_rows(fields, even):
    r, lane = iota((16, 384), 0), iota((16, 384), 1)
    north = (r < 2) == even
    target = jnp.where(north, BAND - 1 - r % 2, r % 2)
    pick = jnp.where((lane == target) & (r < 4), 1.0, 0.0).astype(BF16)
    high, low = split(fields)
    return dot(pick, high, NT) + dot(pick, low, NT)


def placed_rows(first_ref, second_ref, rows_ref, even, polar):
    rows_ref[...] = jnp.zeros_like(rows_ref)
    rows_ref[0:2, :] = first_ref[...]
    wind = iota((2, 1152), 1) < 768
    second = second_ref[...]
    rows_ref[2:4, :] = jnp.where(wind & polar, -second, second)
    r, lane = iota((16, 384), 0), iota((16, 384), 1)
    north = (r < 2) == even
    target = jnp.where(north, BAND + r % 2, 383 - r % 2)
    put = jnp.where((lane == target) & (r < 4), 1.0, 0.0).astype(BF16)
    high, low = split(rows_ref[...])
    return dot(high, put, TN) + dot(low, put, TN)


def lat_of(ids_ref):
    b = ids_ref[0]
    return b, b % 2 == 0, (b == 0) | (b == 3)


def shift_lanes(x, by):
    return pltpu.roll(x, by % x.shape[-1], x.ndim - 1)


def edges_kernel(ids_ref, u_ref, v_ref, p_ref, east_ref, west_ref, first_ref, second_ref, box_ref):
    _, even, _ = lat_of(ids_ref)
    box_ref[...] = jnp.zeros_like(box_ref)
    for f, ref in enumerate((u_ref, v_ref, p_ref)):
        box_ref[f, :, 0:SEG, 0:BAND] = ref[0]
    send_edges(box_ref, (0, 1, 2), even, east_ref, west_ref, first_ref, second_ref)


def send_edges(box_ref, uvp, even, east_ref, west_ref, first_ref, second_ref):
    u, v, p = uvp
    for slot, (f, col) in enumerate(((p, 43), (p, 44), (u, 44), (v, 44))):
        east_ref[slot] = box_ref[f, :, col, :]
    for slot, (f, col) in enumerate(((p, 1), (p, 0), (u, 0), (v, 0))):
        west_ref[slot] = box_ref[f, :, col, :]
    fields = jnp.concatenate([box_ref[f].reshape(384, 384) for f in uvp], axis=0)
    rows = edge_rows(fields, even)
    first_ref[...] = rows[0:2]
    second_ref[...] = rows[2:4]


def fill_columns(ext_ref, from_west_ref, from_east_ref):
    ext_ref[2, :, 6, :] = from_west_ref[0]
    ext_ref[2, :, 7, :] = from_west_ref[1]
    ext_ref[0, :, 7, :] = from_west_ref[2]
    ext_ref[1, :, 7, :] = from_west_ref[3]
    ext_ref[2, :, 54, :] = from_east_ref[0]
    ext_ref[2, :, 53, :] = from_east_ref[1]
    ext_ref[0, :, 53, :] = from_east_ref[2]
    ext_ref[1, :, 53, :] = from_east_ref[3]


def first_kernel(
    ids_ref, state_ref, from_west_ref, from_east_ref, got_first_ref, got_second_ref, tab_ref,
    out_ref, east_ref, west_ref, first_ref, second_ref, ext_ref, rows_ref, w_ref,
):
    _, even, polar = lat_of(ids_ref)
    placed = placed_rows(got_first_ref, got_second_ref, rows_ref, even, polar)
    ext_ref[...] = jnp.zeros_like(ext_ref)
    ext_ref[:, :, 8:56, :] = placed.reshape(3, LEV, 48, 384)
    for f, field in enumerate((0, 1, 3)):
        ext_ref[f, :, 8 : 8 + SEG, 0:BAND] = state_ref[field]
    fill_columns(ext_ref, from_west_ref, from_east_ref)
    a, f, c, qc = (tab_ref[n : n + 1, :] for n in range(4))
    w_ref[...] = jnp.zeros_like(w_ref)
    for lev in range(LEV):
        new_w = state_ref[2, lev] + 0.3 * state_ref[4, lev]
        if lev + 1 < LEV:
            new_w -= 0.25 * state_ref[3, lev + 1]
        if lev > 0:
            new_w += 0.25 * state_ref[3, lev - 1]
        w_ref[lev, 0:SEG, 0:BAND] = new_w
    keep = (iota((48, 384), 0) < SEG) & (iota((48, 384), 1) < BAND)
    for lev in range(LEV):
        u = ext_ref[0, lev, 7:55, :]
        v = ext_ref[1, lev, 7:55, :]
        new_u = u - (0.5 * a) * (ext_ref[2, lev, 8:56, :] - ext_ref[2, lev, 6:54, :]) + f * v
        ext_ref[0, lev, 7:55, :] = new_u
        uc = (u, v)
        del uc
        p = ext_ref[2, lev, 8:56, :]
        old_v = ext_ref[1, lev, 8:56, :]
        old_u = u[1:, :]
        old_u = jnp.concatenate([old_u, u[0:1, :]], axis=0)
        new_v = old_v - 0.25 * (shift_lanes(p, -1) - shift_lanes(p, 1)) - f * old_u
        flux = c * new_v
        new_p = p - (0.5 * a) * (ext_ref[0, lev, 9:57, :] - ext_ref[0, lev, 7:55, :])
        new_p -= qc * (shift_lanes(flux, -1) - shift_lanes(flux, 1))
        if lev + 1 < LEV:
            new_p -= 0.25 * w_ref[lev + 1]
        if lev > 0:
            new_p += 0.25 * w_ref[lev - 1]
        out_ref[0, lev] = jnp.where(keep, ext_ref[0, lev, 8:56, :], 0.0)
        out_ref[1, lev] = jnp.where(keep, new_v, 0.0)
        out_ref[2, lev] = w_ref[lev]
        out_ref[3, lev] = jnp.where(keep, new_p, 0.0)
        out_ref[4, lev] = jnp.zeros((48, 384), F32)
        out_ref[4, lev, 0:SEG, 0:BAND] = state_ref[4, lev] - 0.3 * w_ref[lev, 0:SEG, 0:BAND]
    send_edges(out_ref, (0, 1, 3), even, east_ref, west_ref, first_ref, second_ref)


def row_lanes(ids_ref, rows_ref, index):
    b = ids_ref[0]
    at = jnp.where(b >= 2, FROWS, 0)
    lane = jnp.full(index.shape, -1, I32)
    for k in range(FROWS):
        e = rows_ref[at + k] - BAND * b
        e = jnp.where(e < 0, jnp.where(e >= -2, e + 384, -1), jnp.where(e <= BAND + 1, e, -1))
        lane = jnp.where(index == k, e, lane)
    return lane


def pack_kernel(
    ids_ref, rows_ref, r_ref, got_first_ref, got_second_ref, tab_ref, slot_ref,
    out_ref, next_ref, x_ref, edge_ref,
):
    _, even, polar = lat_of(ids_ref)
    placed = placed_rows(got_first_ref, got_second_ref, edge_ref, even, polar).reshape(3, LEV, 48, 384)
    a, f, c, qc = (tab_ref[n : n + 1, :] for n in range(4))
    for lev in range(LEV):
        new_w = r_ref[2, lev] + 0.3 * r_ref[4, lev]
        if lev + 1 < LEV:
            new_w -= 0.25 * r_ref[3, lev + 1]
        if lev > 0:
            new_w += 0.25 * r_ref[3, lev - 1]
        next_ref[1, lev] = new_w
    for lev in range(LEV):
        u = r_ref[0, lev] + placed[0, lev]
        v = r_ref[1, lev] + placed[1, lev]
        p = r_ref[3, lev] + placed[2, lev]
        g = v - f * u
        new_v = g - 0.25 * (shift_lanes(p, -1) - shift_lanes(p, 1))
        flux = c * new_v
        new_p = p - qc * (shift_lanes(flux, -1) - shift_lanes(flux, 1))
        if lev + 1 < LEV:
            new_p -= 0.25 * next_ref[1, lev + 1]
        if lev > 0:
            new_p += 0.25 * next_ref[1, lev - 1]
        new_w = next_ref[1, lev]
        new_t = r_ref[4, lev] - 0.3 * new_w
        next_ref[0, lev] = new_v
        next_ref[2, lev] = new_p
        next_ref[3, lev] = new_t
        at = pl.ds(48 * lev, 48)
        for n, value in enumerate((p, g, u + f * v, new_v, new_w, new_p, new_t)):
            high, low = split(value)
            x_ref[0, at, 384 * n : 384 * n + 384] = high
            x_ref[1, at, 384 * n : 384 * n + 384] = low
    lane = row_lanes(ids_ref, rows_ref, slot_ref[0:1, :])
    kind = slot_ref[1:2, :]
    row = iota((384, 512), 0)
    one_hot = jnp.concatenate(
        [jnp.where(row == jnp.where(kind == n, lane, -1), 1.0, 0.0).astype(BF16) for n in range(7)],
        axis=0,
    )
    got = dot(x_ref[0], one_hot) + dot(x_ref[1], one_hot)
    low_half = iota((24, 128), 1) < 64
    for lev in range(LEV):
        for t in range(4):
            tile = got[48 * lev : 48 * lev + 48, 128 * t : 128 * t + 128]
            top, bottom = tile[0:24], tile[24:48]
            out_ref[8 * lev + 2 * t] = jnp.where(low_half, top, shift_lanes(bottom, 64))
            out_ref[8 * lev + 2 * t + 1] = jnp.where(low_half, shift_lanes(top, 64), bottom)


def zonal_kernel(r_ref, p2_ref, from_west_ref, from_east_ref, tab_ref, out_ref, ext_ref):
    a, f = tab_ref[0:1, :], tab_ref[1:2, :]
    ext_ref[:, :, 0:8, :] = jnp.zeros((3, LEV, 8, 384), F32)
    ext_ref[:, :, 56:64, :] = jnp.zeros((3, LEV, 8, 384), F32)
    for n, field in enumerate((0, 1, 3)):
        ext_ref[n, :, 8:56, :] = r_ref[field]
    fill_columns(ext_ref, from_west_ref, from_east_ref)
    for lev in range(LEV):
        new_u = (
            ext_ref[0, lev, 7:55, :]
            - (0.5 * a) * (ext_ref[2, lev, 8:56, :] - ext_ref[2, lev, 6:54, :])
            + f * ext_ref[1, lev, 7:55, :]
        )
        ext_ref[0, lev, 7:55, :] = new_u
        out_ref[0, lev] = ext_ref[0, lev, 8:56, :]
        out_ref[1, lev] = p2_ref[2, lev] - (0.5 * a) * (
            ext_ref[0, lev, 9:57, :] - ext_ref[0, lev, 7:55, :]
        )


def spectral_kernel(
    ids_ref, rows_ref, cut_ref, cos_ref, in_ref, slot_ref, fwd_ref, mf_ref, mi2_ref, mi1_ref, inv_ref, sig_ref,
    out_ref, z_ref, y_ref, mix_ref,
):
    b, owner = ids_ref[0], ids_ref[1]
    at = jnp.where(b >= 2, FROWS, 0)
    first = 8 * (owner % 8)
    low_half = iota((96, 128), 1) < 64
    for r in range(0, 24, 2):
        high0, low0 = split(in_ref[:, r, :])
        high1, low1 = split(in_ref[:, r + 1, :])
        both = jnp.concatenate(
            [
                jnp.concatenate([high0, high0, low0], axis=0),
                jnp.concatenate([high1, high1, low1], axis=0),
            ],
            axis=1,
        )
        z = dot(fwd_ref[...], both)
        for n in range(2):
            part = z[:, 128 * n : 128 * n + 128]
            z_ref[:, r + n, :] = part[0:40]
            z_ref[:, 24 + r + n, :] = part[40:80]
    rho = slot_ref[2:3, 0:128]
    kind = slot_ref[3:4, 0:128]

    def listed(k):
        return jnp.where((k >= 0) & (k < FROWS), rows_ref[at + jnp.clip(k, 0, FROWS - 1)], -1000)

    row_at = [listed(first + t) for t in range(-4, 12)]
    cut_at = [cut_ref[at + jnp.clip(first + t, 0, FROWS - 1)] for t in range(-4, 12)]
    blank = jnp.zeros((1, 128), F32)
    rows = [jnp.full((1, 128), -1000, I32) for _ in range(5)]
    cut, c0, cp, cm = jnp.zeros((1, 128), I32), blank + 1.0, blank, blank
    for t in range(-2, 10):
        here = rho == t
        j = row_at[t + 4]
        jc = jnp.clip(j, 0, NLAT - 1)
        for d in range(-2, 3):
            rows[d + 2] = jnp.where(here, row_at[t + d + 4], rows[d + 2]) if 0 <= t + d + 4 < 16 else rows[d + 2]
        cut = jnp.where(here, cut_at[t + 4], cut)
        cm = jnp.where(here, cos_ref[jc], cm)
        c0 = jnp.where(here, cos_ref[jc + 1], c0)
        cp = jnp.where(here, cos_ref[jc + 2], cp)
    j = rows[2]

    def yes(cond):
        return jnp.where(cond, 1.0, 0.0)

    up1, dn1 = yes(rows[3] == j + 1), yes(rows[1] == j - 1)
    up2, up22 = yes(rows[3] == j + 2), yes(rows[4] == j + 2)
    dn2, dn22 = yes(rows[1] == j - 2), yes(rows[0] == j - 2)
    south, north = yes(j == 0), yes(j == NLAT - 1)
    a = 0.5 * cos_ref[1] / c0
    qc = -0.25 / c0
    src, dst = iota((128, 128), 0), iota((128, 128), 1)

    def mix(terms):
        total = jnp.zeros((128, 128), F32)
        for to, shift, coef in terms:
            total = jnp.where(src == dst - shift, jnp.where(kind == to, coef, 0.0), total) if False else (
                total + jnp.where((src == dst - shift) & (kind == to), coef, 0.0)
            )
        return total

    on_d = mix([(2, 20, -a), (5, 24, -a)])
    on_s = mix([(5, 44, -a * a)])
    q0 = -0.25 * (cp * (1 - north) + cm * (1 - south) + c0 * (south + north))
    on_h = mix(
        [
            (1, 10, 0.25 * up1), (1, 12, -0.25 * dn1),
            (3, 27, 0.25 * up1), (3, 29, -0.25 * dn1), (3, 17, blank - 1.0),
            (5, 44, qc * q0),
            (5, 43, qc * 0.25 * cp * up2), (5, 42, qc * 0.25 * cp * up22),
            (5, 45, qc * 0.25 * cm * dn2), (5, 46, qc * 0.25 * cm * dn22),
            (5, 32, -qc * cp * up1), (5, 34, qc * cm * dn1),
        ]
    )
    pole = 0.25 * (north - south)
    on_p = mix(
        [
            (1, 11, pole), (3, 28, pole),
            (5, 43, qc * 0.25 * (cp * yes(j == NLAT - 2) + c0 * south * up1)),
            (5, 45, qc * 0.25 * (cm * yes(j == 1) + c0 * north * dn1)),
            (5, 33, qc * c0 * (north - south)),
        ]
    )
    for n, m in enumerate((on_d, on_s, on_h, on_p)):
        high, low = split(m)
        mix_ref[0, 128 * n : 128 * n + 128, :] = high
        mix_ref[1, 128 * n : 128 * n + 128, :] = low
    final = kind >= 2
    sign = jnp.where(kind == 1, -1.0, 1.0)
    k_base = 64 * (iota((96, 128), 0) % 48) + jnp.where(low_half, 0, PAIRS)
    odd_base = jnp.where(iota((96, 128), 1) < 64, 1.0, -1.0)
    y_ref[PAIRS:24] = jnp.zeros((24 - PAIRS, 96, 128), F32)
    for pair in range(PAIRS):
        parts = []
        for half in range(2):
            q = pair + PAIRS * half
            high, low = split(z_ref[q])
            got = dot(mf_ref[q], jnp.concatenate([high, high, low], axis=0))
            parts.append(got)
        s = jnp.where(
            low_half,
            parts[0][0:96] + shift_lanes(parts[0][96:192], 64),
            shift_lanes(parts[1][0:96], 64) + parts[1][96:192],
        )
        k = k_base + pair
        keep = jnp.minimum(k, NLON - k) <= cut
        h = jnp.where(keep, 0.0, s)
        sig = sig_ref[pair]
        d = sig * jnp.concatenate([s[48:96], s[0:48]], axis=0)
        ph = (odd_base if pair % 2 == 0 else -odd_base) * h
        terms = jnp.concatenate([d, sig * sig * s, h, ph], axis=1)
        high, low = split(terms)
        corr = dot(high, mix_ref[0]) + dot(low, mix_ref[0]) + dot(high, mix_ref[1])
        t = jnp.where(final, jnp.where(keep, s + corr, 0.0), sign * h + corr)
        high, low = split(t)
        back = dot(mi2_ref[pair], jnp.concatenate([high, high], axis=0)) + dot(mi1_ref[pair], low)
        y_ref[pair] = jnp.where(low_half, back[0:96], back[96:192])
    half64 = iota((64, 128), 1) < 64
    for r in range(24):
        cols = []
        for i in (r, r + 24):
            zz = jnp.concatenate([y_ref[:, i, :], y_ref[:, 48 + i, :]], axis=0)
            high, low = split(zz)
            cols.append(jnp.concatenate([high, high, low], axis=0))
        x = dot(inv_ref[...], jnp.concatenate(cols, axis=1))
        out_ref[:, r, :] = jnp.where(
            half64,
            x[0:64, 0:128] + shift_lanes(x[64:128, 0:128], 64),
            shift_lanes(x[0:64, 128:256], 64) + x[64:128, 128:256],
        )


def final_kernel(ids_ref, rows_ref, in_ref, next_ref, zonal_ref, tab_ref, slot_ref, out_ref, b_ref):
    low_half = iota((24, 128), 1) < 64
    for lev in range(LEV):
        for t in range(4):
            even, odd = in_ref[8 * lev + 2 * t], in_ref[8 * lev + 2 * t + 1]
            tile = jnp.concatenate(
                [
                    jnp.where(low_half, even, shift_lanes(odd, 64)),
                    jnp.where(low_half, shift_lanes(even, 64), odd),
                ],
                axis=0,
            )
            high, low = split(tile)
            b_ref[0, 48 * lev : 48 * lev + 48, 128 * t : 128 * t + 128] = high
            b_ref[1, 48 * lev : 48 * lev + 48, 128 * t : 128 * t + 128] = low
    index = slot_ref[0:1, :]
    rho = slot_ref[2:3, :]
    own = (rho >= 0) & (rho < 8)
    lane = row_lanes(ids_ref, rows_ref, index)
    kind = slot_ref[1:2, :]
    row = iota((384, 512), 0)

    def spread(n):
        one_hot = jnp.where(row == jnp.where((kind == n) & own, lane, -1), 1.0, 0.0).astype(BF16)
        return dot(b_ref[0], one_hot, NT) + dot(b_ref[1], one_hot, NT)

    flag = jnp.zeros((1, 384), F32)
    at = jnp.where(ids_ref[0] >= 2, FROWS, 0)
    lanes = iota((1, 384), 1)
    for k in range(FROWS):
        e = rows_ref[at + k] - BAND * ids_ref[0]
        e = jnp.where((e < 0) & (e >= -2), e + 384, e)
        flag = jnp.where(lanes == e, 1.0, flag)
    flagged = flag > 0.5
    inner = flagged[:, 0:BAND]
    c, qc = tab_ref[2:3, :], tab_ref[3:4, :]
    hp, dv = spread(0), spread(1)
    dv = jnp.where(flagged, dv, 0.25 * (shift_lanes(hp, -1) - shift_lanes(hp, 1)))
    flux = c * dv
    dp = -qc * (shift_lanes(flux, -1) - shift_lanes(flux, 1))
    sources = (
        (0, 2, lambda lev: zonal_ref[0, lev]),
        (1, 3, lambda lev: next_ref[0, lev] + dv[48 * lev : 48 * lev + 48]),
        (2, 4, lambda lev: next_ref[1, lev]),
        (3, 5, lambda lev: zonal_ref[1, lev] + dp[48 * lev : 48 * lev + 48]),
        (4, 6, lambda lev: next_ref[3, lev]),
    )
    for field, n, plain in sources:
        filtered = spread(n)
        for lev in range(LEV):
            out_ref[field, lev] = jnp.where(
                inner, filtered[48 * lev : 48 * lev + SEG, 0:BAND], plain(lev)[0:SEG, 0:BAND]
            )


VMEM = pl.BlockSpec(memory_space=pltpu.VMEM)
SMEM = pl.BlockSpec(memory_space=pltpu.SMEM)


def call(body, name, n_smem, args, outs, scratch, flops, mib):
    return pl.pallas_call(
        body,
        name=name,
        out_shape=outs,
        in_specs=[SMEM] * n_smem + [VMEM] * (len(args) - n_smem),
        out_specs=jax.tree.map(lambda _: VMEM, outs),
        scratch_shapes=scratch,
        compiler_params=pltpu.CompilerParams(vmem_limit_bytes=mib << 20),
        cost_estimate=pl.CostEstimate(flops=flops, bytes_accessed=8 << 20, transcendentals=0),
    )(*args)


def shape(*dims):
    return jax.ShapeDtypeStruct(dims, F32)


def neighbours():
    first, second = [], []
    for l in range(64):
        for b in (0, 2):
            first += [(64 * b + l, 64 * b + 64 + l), (64 * b + 64 + l, 64 * b + l)]
        second += [(64 + l, 128 + l), (128 + l, 64 + l)]
        second += [(l, (l + 32) % 64), (192 + l, 192 + (l + 32) % 64)]
    return first, second


def exchange(edges):
    east, west, first, second = edges
    pairs_first, pairs_second = neighbours()
    got_first = lax.ppermute(first, ("lat", "lon"), pairs_first)
    got_second = lax.ppermute(second, ("lat", "lon"), pairs_second)
    from_west = lax.ppermute(east, "lon", [(i, (i + 1) % 64) for i in range(64)])
    from_east = lax.ppermute(west, "lon", [((i + 1) % 64, i) for i in range(64)])
    return from_west, from_east, got_first, got_second


def row_tables(b):
    def cosine(row):
        return jnp.abs(jnp.sin((row.astype(F32) + 0.5) * (jnp.pi / NLAT)))

    lane = jnp.arange(384, dtype=I32)
    row = jnp.where(lane < 370, lane, lane - 384) + BAND * b
    c = cosine(row)
    f = -0.2 * jnp.cos((row.astype(F32) + 0.5) * (jnp.pi / NLAT))
    polar = cosine(jnp.zeros((), I32))
    zero = jnp.zeros_like(c)
    tab = jnp.stack([0.5 * polar / c, f, c, 0.25 / c, zero, zero, zero, zero])
    return tab, cosine(jnp.arange(-1, 1447, dtype=I32))


def per_device(prognostic, filter_rows, cutoff):
    b, lon = lax.axis_index("lat"), lax.axis_index("lon")
    ids = jnp.stack([b, lon]).astype(I32)
    tab, cosines = row_tables(b)
    rho64, kind64 = slot_tables()
    slots = np.full((8, 512), -1, np.int32)
    slots[0] = (8 * np.arange(8)[:, None] + rho64[None, :]).reshape(-1)
    slots[1] = np.tile(kind64, 8)
    slots[2] = np.tile(rho64, 8)
    slots[3] = np.tile(kind64, 8)
    margin = (slots[2] < 0) | (slots[2] > 7)
    slots[3] = np.where(margin & (slots[1] == 1), 0, slots[3])
    slots = jnp.asarray(slots)
    fwd, mf, mi2, mi1, inv, sig = (jnp.asarray(x) for x in fourier_constants())

    edge_shapes = (shape(4, 8, 384), shape(4, 8, 384), shape(2, 1152), shape(2, 1152))
    winds = [prognostic[n : n + 1] for n in (0, 1, 3)]
    edges = call(
        edges_kernel, "edges", 1, (ids, *winds), edge_shapes,
        [pltpu.VMEM((3, 8, 48, 384), F32)], 10**7, 16,
    )
    state, *edges = call(
        first_kernel, "first", 1, (ids, prognostic, *exchange(edges), tab),
        (shape(5, 8, 48, 384), *edge_shapes),
        [pltpu.VMEM((3, 8, 64, 384), F32), pltpu.VMEM((16, 1152), F32), pltpu.VMEM((8, 48, 384), F32)],
        10**8, 24,
    )
    from_west, from_east, got_first, got_second = exchange(edges)
    message, after = call(
        pack_kernel, "pack", 2,
        (ids, filter_rows, state, got_first, got_second, tab, slots),
        (shape(64, 24, 128), shape(4, 8, 48, 384)),
        [pltpu.VMEM((2, 384, 2688), BF16), pltpu.VMEM((16, 1152), F32)], 10**9, 32,
    )
    whole = lax.all_to_all(message, "lon", split_axis=0, concat_axis=0, tiled=True)
    zonal = call(
        zonal_kernel, "zonal", 0, (state, after, from_west, from_east, tab),
        shape(2, 8, 48, 384), [pltpu.VMEM((3, 8, 64, 384), F32)], 10**8, 16,
    )
    answer = call(
        spectral_kernel, "spectral", 4,
        (ids, filter_rows, cutoff, cosines, whole, slots, fwd, mf, mi2, mi1, inv, sig),
        shape(64, 24, 128),
        [pltpu.VMEM((40, 48, 128), F32), pltpu.VMEM((24, 96, 128), F32), pltpu.VMEM((2, 512, 128), BF16)],
        10**9, 24,
    )
    back = lax.all_to_all(answer, "lon", split_axis=0, concat_axis=0, tiled=True)
    return call(
        final_kernel, "final", 2, (ids, filter_rows, back, after, zonal, tab, slots),
        shape(5, 8, 45, 360), [pltpu.VMEM((2, 384, 512), BF16)], 10**9, 32,
    )


def solution(mesh):
    in_specs = (P(None, None, "lon", "lat"), P(), P())
    out_specs = P(None, None, "lon", "lat")
    return jax.shard_map(
        per_device, mesh=mesh, in_specs=in_specs, out_specs=out_specs, check_vma=False
    )
```

```python
import jax
import jax.numpy as jnp
import ml_dtypes
import numpy as np
from jax import lax
from jax.experimental import pallas as pl
from jax.experimental.pallas import tpu as pltpu
from jax.sharding import PartitionSpec as P

NLON, NLAT, LEV = 2880, 1440, 8
SEG, BAND, FROWS, FIELDS = 45, 360, 64, 5
F32, BF16, I32 = jnp.float32, jnp.bfloat16, jnp.int32
NN = (((1,), (0,)), ((), ()))
NT = (((1,), (1,)), ((), ()))
TN = (((0,), (0,)), ((), ()))

SLOT_BASE = (0, 12, 22, 30, 38, 46, 54)
SLOT_COUNT = (12, 10, 8, 8, 8, 8, 8)
SLOT_FIRST = (-2, -1, 0, 0, 0, 0, 0)
PAIRS = 17
MROWS = 23
COLS = 2 * MROWS
EDGE = 3 * SEG * LEV


def slot_tables():
    rho = np.full(64, -100, np.int32)
    kind = np.full(64, -1, np.int32)
    for f, (base, count, first) in enumerate(zip(SLOT_BASE, SLOT_COUNT, SLOT_FIRST)):
        rho[base : base + count] = first + np.arange(count)
        kind[base : base + count] = f
    return rho, kind


def split_np(m):
    high = m.astype(ml_dtypes.bfloat16)
    low = (m - high.astype(np.float64)).astype(ml_dtypes.bfloat16)
    return high, low


def triple(m):
    high, low = split_np(m)
    return np.concatenate([high, low, high], axis=-1)


def fourier_constants():
    s = np.arange(64)
    k1 = np.arange(33)
    ang = 2 * np.pi * (np.outer(k1, s) % 64) / 64
    fwd = np.zeros((80, 64))
    fwd[:33], fwd[40:73] = np.cos(ang), -np.sin(ang)
    inv = np.zeros((2, 64, 2, 24))
    sig = np.zeros((PAIRS, 96, 128))
    mf = np.zeros((2 * PAIRS, 192, 48))
    mi = np.zeros((PAIRS, 192, 96))
    i, k2 = np.arange(SEG), np.arange(SEG)
    for q in range(33):
        half, pair = divmod(q, PAIRS)
        inv[half, :, 0, pair] = np.cos(ang[q])
        inv[half, :, 1, pair] = -np.sin(ang[q])
        k = q + 64 * k2
        w = 2 * np.pi * (np.outer(k, i) % NLON) / NLON
        full = np.zeros((2, 48, 2, 48))
        full[0, :SEG, 0, :SEG], full[0, :SEG, 1, :SEG] = np.cos(w), np.sin(w)
        full[1, :SEG, 0, :SEG], full[1, :SEG, 1, :SEG] = -np.sin(w), np.cos(w)
        for h in range(2):
            mf[q, 96 * h : 96 * h + 96] = np.stack([np.pad(full[:, :, n, h : 2 * MROWS : 2], ((0, 0), (0, 0), (0, 1))) for n in range(2)], axis=2).reshape(96, 48)
        scale = (1.0 if q in (0, 32) else 2.0) / NLON
        mi[pair, 96 * half : 96 * half + 96] = full.reshape(96, 96).T * scale
        sn = np.sin(2 * np.pi * k / NLON)
        sig[pair, :SEG, 64 * half : 64 * half + 64] = -sn[:, None]
        sig[pair, 48 : 48 + SEG, 64 * half : 64 * half + 64] = sn[:, None]
    return (
        triple(fwd),
        triple(inv.reshape(128, 48)),
        np.concatenate(split_np(mf), axis=-1),
        np.concatenate(split_np(mi), axis=-1),
        sig.astype(np.float32),
    )


def dot(a, b, dims=NN):
    return lax.dot_general(a, b, dims, preferred_element_type=F32)


def split(x):
    high = x.astype(BF16)
    return high, (x - high.astype(F32)).astype(BF16)


def iota(shape, axis):
    return lax.broadcasted_iota(I32, shape, axis)


def edge_rows(fields, even):
    r, lane = iota((16, 384), 0), iota((16, 384), 1)
    north = (r < 2) == even
    target = jnp.where(north, BAND - 1 - r % 2, r % 2)
    pick = jnp.where((lane == target) & (r < 4), 1.0, 0.0).astype(BF16)
    high, low = split(fields)
    return dot(pick, high, NT) + dot(pick, low, NT)


def placed_rows(first_ref, second_ref, rows_ref, even, polar):
    rows_ref[...] = jnp.zeros_like(rows_ref)
    rows_ref[0:2, :] = first_ref[...]
    wind = iota((2, EDGE), 1) < 720
    second = second_ref[...]
    rows_ref[2:4, :] = jnp.where(wind & polar, -second, second)
    r, lane = iota((16, 384), 0), iota((16, 384), 1)
    north = (r < 2) == even
    target = jnp.where(north, BAND + r % 2, 383 - r % 2)
    put = jnp.where((lane == target) & (r < 4), 1.0, 0.0).astype(BF16)
    high, low = split(rows_ref[...])
    return (dot(high, put, TN) + dot(low, put, TN)).reshape(3, SEG, LEV, 384)


def lat_of(ids_ref):
    b = ids_ref[0]
    return b, b % 2 == 0, (b == 0) | (b == 3)


def shift_lanes(x, by):
    return pltpu.roll(x, by % x.shape[-1], x.ndim - 1)


def level_difference(x):
    lev = iota(x.shape, x.ndim - 2)
    above = jnp.where(lev < LEV - 1, pltpu.roll(x, LEV - 1, x.ndim - 2), 0.0)
    below = jnp.where(lev > 0, pltpu.roll(x, 1, x.ndim - 2), 0.0)
    return above - below


def row_difference(x):
    return shift_lanes(x, -1) - shift_lanes(x, 1)


def edges_kernel(ids_ref, state_ref, east_ref, west_ref, first_ref, second_ref, box_ref):
    _, even, _ = lat_of(ids_ref)
    box_ref[:, :, :, 256:384] = jnp.zeros((3, SEG, LEV, 128), F32)
    for n, field in enumerate((0, 1, 3)):
        box_ref[n, :, :, 0:BAND] = state_ref[field]
    send_edges(box_ref, (0, 1, 2), even, east_ref, west_ref, first_ref, second_ref)


def send_edges(box_ref, uvp, even, east_ref, west_ref, first_ref, second_ref):
    u, v, p = uvp
    for slot, (f, col) in enumerate(((p, 43), (p, 44), (u, 44), (v, 44))):
        east_ref[slot] = box_ref[f, col]
    for slot, (f, col) in enumerate(((p, 1), (p, 0), (u, 0), (v, 0))):
        west_ref[slot] = box_ref[f, col]
    fields = jnp.concatenate([box_ref[f].reshape(360, 384) for f in uvp], axis=0)
    rows = edge_rows(fields, even)
    first_ref[...] = rows[0:2]
    second_ref[...] = rows[2:4]


def fill_columns(ext_ref, from_west_ref, from_east_ref):
    ext_ref[2, 0] = from_west_ref[0]
    ext_ref[2, 1] = from_west_ref[1]
    ext_ref[0, 1] = from_west_ref[2]
    ext_ref[1, 1] = from_west_ref[3]
    ext_ref[2, 48] = from_east_ref[0]
    ext_ref[2, 47] = from_east_ref[1]
    ext_ref[0, 47] = from_east_ref[2]
    ext_ref[1, 47] = from_east_ref[3]


CHUNKS = tuple((i, min(i + 5, SEG)) for i in range(0, SEG, 5))


def first_kernel(
    ids_ref, state_ref, from_west_ref, from_east_ref, got_first_ref, got_second_ref, tab_ref,
    out_ref, east_ref, west_ref, first_ref, second_ref, ext_ref, rows_ref, new_u_ref,
):
    _, even, polar = lat_of(ids_ref)
    ext_ref[:, 2:47] = placed_rows(got_first_ref, got_second_ref, rows_ref, even, polar)
    for n, field in enumerate((0, 1, 3)):
        ext_ref[n, 2:47, :, 0:BAND] = state_ref[field]
    fill_columns(ext_ref, from_west_ref, from_east_ref)
    a, f, c, qc = (tab_ref[n : n + 1, :] for n in range(4))
    out_ref[:, :, :, 256:384] = jnp.zeros((5, SEG, LEV, 128), F32)
    for i, end in ((-1, 0), *CHUNKS, (45, 46)):
        new_u_ref[i + 1 : end + 1] = (
            ext_ref[0, i + 2 : end + 2]
            - (0.5 * a) * (ext_ref[2, i + 3 : end + 3] - ext_ref[2, i + 1 : end + 1])
            + f * ext_ref[1, i + 2 : end + 2]
        )
    for i, end in CHUNKS:
        at = slice(i + 2, end + 2)
        p = ext_ref[2, at]
        new_v = ext_ref[1, at] - 0.25 * row_difference(p) - f * ext_ref[0, at]
        new_p = p - (0.5 * a) * (new_u_ref[i + 2 : end + 2] - new_u_ref[i:end])
        new_p -= qc * row_difference(c * new_v)
        th = state_ref[4, i:end]
        new_w = state_ref[2, i:end] - 0.25 * level_difference(state_ref[3, i:end]) + 0.3 * th
        out_ref[0, i:end, :, 0:BAND] = new_u_ref[i + 1 : end + 1, :, 0:BAND]
        out_ref[1, i:end, :, 0:BAND] = new_v[:, :, 0:BAND]
        out_ref[2, i:end, :, 0:BAND] = new_w
        out_ref[3, i:end, :, 0:BAND] = new_p[:, :, 0:BAND] - 0.25 * level_difference(new_w)
        out_ref[4, i:end, :, 0:BAND] = th - 0.3 * new_w
    send_edges(out_ref, (0, 1, 3), even, east_ref, west_ref, first_ref, second_ref)


def row_lanes(ids_ref, rows_ref, index):
    b = ids_ref[0]
    at = jnp.where(b >= 2, FROWS, 0)
    lane = jnp.full(index.shape, -1, I32)
    for k in range(FROWS):
        e = rows_ref[at + k] - BAND * b
        e = jnp.where(e < 0, jnp.where(e >= -2, e + 384, -1), jnp.where(e <= BAND + 1, e, -1))
        lane = jnp.where(index == k, e, lane)
    return lane


def pack_kernel(
    ids_ref, rows_ref, r_ref, got_first_ref, got_second_ref, tab_ref, slot_ref,
    out_ref, next_ref, x_ref, edge_ref, placed_ref,
):
    _, even, polar = lat_of(ids_ref)
    placed_ref[...] = placed_rows(got_first_ref, got_second_ref, edge_ref, even, polar)
    a, f, c, qc = (tab_ref[n : n + 1, :] for n in range(4))
    for i in range(0, SEG, 6):
        end = min(i + 6, SEG)
        at = slice(i, end)
        u = r_ref[0, at] + placed_ref[0, at]
        v = r_ref[1, at] + placed_ref[1, at]
        p = r_ref[3, at] + placed_ref[2, at]
        th = r_ref[4, at]
        g = v - f * u
        new_v = g - 0.25 * row_difference(p)
        new_w = r_ref[2, at] - 0.25 * level_difference(p) + 0.3 * th
        new_p = p - qc * row_difference(c * new_v) - 0.25 * level_difference(new_w)
        new_t = th - 0.3 * new_w
        for n, value in enumerate((new_v, new_w, new_p, new_t)):
            next_ref[n, at] = value
        rows = slice(LEV * i, LEV * (end + (end - i) % 2))
        for n, value in enumerate((p, g, u + f * v, new_v, new_w, new_p, new_t)):
            if (end - i) % 2:
                value = jnp.concatenate([value, jnp.zeros((1, LEV, 384), F32)], axis=0)
            high, low = split(value.reshape(-1, 384))
            x_ref[0, rows, 384 * n : 384 * n + 384] = high
            x_ref[1, rows, 384 * n : 384 * n + 384] = low
    lane = row_lanes(ids_ref, rows_ref, slot_ref[0:1, :])
    kind = slot_ref[1:2, :]
    row = iota((384, 512), 0)
    one_hot = jnp.concatenate(
        [jnp.where(row == jnp.where(kind == n, lane, -1), 1.0, 0.0).astype(BF16) for n in range(7)], axis=0
    )
    got = dot(x_ref[0], one_hot) + dot(x_ref[1], one_hot)
    low_half = iota((8, 128), 1) < 64
    for r in range(MROWS):
        for t in range(4):
            top = got[16 * r : 16 * r + 8, 128 * t : 128 * t + 128]
            bottom = got[16 * r + 8 : 16 * r + 16, 128 * t : 128 * t + 128]
            out_ref[:, 2 * t, r, :] = jnp.where(low_half, top, shift_lanes(bottom, 64))
            out_ref[:, 2 * t + 1, r, :] = jnp.where(low_half, shift_lanes(top, 64), bottom)


def zonal_kernel(r_ref, p2_ref, from_west_ref, from_east_ref, tab_ref, out_ref, ext_ref, new_u_ref):
    a, f = tab_ref[0:1, :], tab_ref[1:2, :]
    for n, field in enumerate((0, 1, 3)):
        ext_ref[n, 2:47] = r_ref[field]
    fill_columns(ext_ref, from_west_ref, from_east_ref)
    for i, end in ((-1, 0), *CHUNKS, (45, 46)):
        new_u_ref[i + 1 : end + 1] = (
            ext_ref[0, i + 2 : end + 2]
            - (0.5 * a) * (ext_ref[2, i + 3 : end + 3] - ext_ref[2, i + 1 : end + 1])
            + f * ext_ref[1, i + 2 : end + 2]
        )
    for i, end in CHUNKS:
        out_ref[0, i:end] = new_u_ref[i + 1 : end + 1]
        out_ref[1, i:end] = p2_ref[2, i:end] - (0.5 * a) * (new_u_ref[i + 2 : end + 2] - new_u_ref[i:end])


def spectral_kernel(
    ids_ref, rows_ref, cut_ref, cos_ref, in_ref, slot_ref, fwd_ref, inv_ref, mf_ref, mi_ref, sig_ref,
    out_ref, z_ref, s_ref, y_ref, mix_ref,
):
    b, owner = ids_ref[0], ids_ref[1]
    at = jnp.where(b >= 2, FROWS, 0)
    first = 8 * (owner % 8)
    low_half = iota((96, 128), 1) < 64

    rho = slot_ref[2:3, 0:128]
    kind = slot_ref[3:4, 0:128]

    def listed(k):
        return jnp.where((k >= 0) & (k < FROWS), rows_ref[at + jnp.clip(k, 0, FROWS - 1)], -1000)

    row_at = [listed(first + t) for t in range(-4, 12)]
    cut_at = [cut_ref[at + jnp.clip(first + t, 0, FROWS - 1)] for t in range(-4, 12)]
    blank = jnp.zeros((1, 128), F32)
    rows = [jnp.full((1, 128), -1000, I32) for _ in range(5)]
    cut, c0, cp, cm = jnp.zeros((1, 128), I32), blank + 1.0, blank, blank
    for t in range(-2, 10):
        here = rho == t
        jc = jnp.clip(row_at[t + 4], 0, NLAT - 1)
        for d in range(-2, 3):
            rows[d + 2] = jnp.where(here, row_at[t + d + 4], rows[d + 2])
        cut = jnp.where(here, cut_at[t + 4], cut)
        cm = jnp.where(here, cos_ref[jc], cm)
        c0 = jnp.where(here, cos_ref[jc + 1], c0)
        cp = jnp.where(here, cos_ref[jc + 2], cp)
    j = rows[2]

    def yes(cond):
        return jnp.where(cond, 1.0, 0.0)

    up1, dn1 = yes(rows[3] == j + 1), yes(rows[1] == j - 1)
    up2, up22 = yes(rows[3] == j + 2), yes(rows[4] == j + 2)
    dn2, dn22 = yes(rows[1] == j - 2), yes(rows[0] == j - 2)
    south, north = yes(j == 0), yes(j == NLAT - 1)
    a = 0.5 * cos_ref[1] / c0
    qc = -0.25 / c0
    src, dst = iota((128, 128), 0), iota((128, 128), 1)

    def mix(n, terms):
        total = jnp.zeros((128, 128), F32)
        for to, shift, coef in terms:
            total += jnp.where(src == dst - shift, jnp.where(kind == to, coef, 0.0), 0.0)
        high, low = split(total)
        mix_ref[128 * n : 128 * n + 128, 0:128] = high
        mix_ref[128 * n : 128 * n + 128, 128:256] = low

    q0 = -0.25 * (cp * (1 - north) + cm * (1 - south) + c0 * (south + north))
    pole = 0.25 * (north - south)
    mix(0, [(2, 20, -a), (5, 24, -a)])
    mix(1, [(5, 44, -a * a)])
    mix(
        2,
        [
            (1, 10, 0.25 * up1), (1, 12, -0.25 * dn1),
            (3, 27, 0.25 * up1), (3, 29, -0.25 * dn1), (3, 17, blank - 1.0),
            (5, 44, qc * q0),
            (5, 43, qc * 0.25 * cp * up2), (5, 42, qc * 0.25 * cp * up22),
            (5, 45, qc * 0.25 * cm * dn2), (5, 46, qc * 0.25 * cm * dn22),
            (5, 32, -qc * cp * up1), (5, 34, qc * cm * dn1),
        ],
    )
    mix(
        3,
        [
            (1, 11, pole), (3, 28, pole),
            (5, 43, qc * 0.25 * (cp * yes(j == NLAT - 2) + c0 * south * up1)),
            (5, 45, qc * 0.25 * (cm * yes(j == 1) + c0 * north * dn1)),
            (5, 33, qc * c0 * (north - south)),
        ],
    )

    z_ref[:, MROWS, :] = jnp.zeros((40, 128), F32)
    z_ref[:, 24 + MROWS, :] = jnp.zeros((40, 128), F32)
    for r in range(0, MROWS, 2):
        pieces = []
        for q in range(r, min(r + 2, MROWS)):
            high, low = split(in_ref[:, q, :])
            pieces.append(jnp.concatenate([high, high, low], axis=0))
        z = dot(fwd_ref[...], pieces[0] if len(pieces) == 1 else jnp.concatenate(pieces, axis=1))
        for n in range(len(pieces)):
            z_ref[:, r + n, :] = z[0:40, 128 * n : 128 * n + 128]
            z_ref[:, 24 + r + n, :] = z[40:80, 128 * n : 128 * n + 128]

    def both_pieces(x):
        high, low = split(x)
        return jnp.concatenate(
            [jnp.concatenate([high, low], axis=1), jnp.concatenate([high, jnp.zeros_like(low)], axis=1)], axis=0
        )

    for pair in range(PAIRS):
        parts = []
        for half in range(2):
            got = dot(mf_ref[pair + PAIRS * half], both_pieces(z_ref[pair + PAIRS * half]))
            parts.append(got[:, 0:128] + got[:, 128:256])
        s_ref[pair] = jnp.where(
            low_half,
            parts[0][0:96] + shift_lanes(parts[0][96:192], 64),
            shift_lanes(parts[1][0:96], 64) + parts[1][96:192],
        )
    final = kind >= 2
    sign = jnp.where(kind == 1, -1.0, 1.0)
    k_base = 64 * (iota((96, 128), 0) % 48) + jnp.where(low_half, 0, PAIRS)
    odd_base = jnp.where(low_half, 1.0, -1.0)
    for pair in range(PAIRS):
        s = s_ref[pair]
        k = k_base + pair
        keep = jnp.minimum(k, NLON - k) <= cut
        h = jnp.where(keep, 0.0, s)
        sig = sig_ref[pair]
        d = sig * jnp.concatenate([s[48:96], s[0:48]], axis=0)
        ph = (odd_base if pair % 2 == 0 else -odd_base) * h
        high, low = split(jnp.concatenate([d, sig * sig * s, h, ph], axis=1))
        corr = dot(high, mix_ref[...])
        corr = corr[:, 0:128] + corr[:, 128:256] + dot(low, mix_ref[:, 0:128])
        s_ref[pair] = jnp.where(final, jnp.where(keep, s + corr, 0.0), sign * h + corr)
    y_ref[PAIRS:24] = jnp.zeros((24 - PAIRS, 96, 128), F32)
    for pair in range(PAIRS):
        back = dot(mi_ref[pair], both_pieces(s_ref[pair]))
        back = back[:, 0:128] + back[:, 128:256]
        y_ref[pair] = jnp.where(low_half, back[0:96], back[96:192])
    half64 = iota((64, 128), 1) < 64
    for r in range(MROWS):
        cols = []
        for i in (2 * r, 2 * r + 1):
            zz = jnp.concatenate([y_ref[:, i, :], y_ref[:, 48 + i, :]], axis=0)
            high, low = split(zz)
            cols.append(jnp.concatenate([high, high, low], axis=0))
        x = dot(inv_ref[...], jnp.concatenate(cols, axis=1))
        out_ref[:, r, :] = jnp.where(
            half64,
            x[0:64, 0:128] + shift_lanes(x[64:128, 0:128], 64),
            shift_lanes(x[0:64, 128:256], 64) + x[64:128, 128:256],
        )


def final_kernel(ids_ref, rows_ref, in_ref, next_ref, zonal_ref, tab_ref, slot_ref, out_ref, piece_ref):
    low_half = iota((8, 128), 1) < 64
    for r in range(MROWS):
        for t in range(4):
            even, odd = in_ref[:, 2 * t, r, :], in_ref[:, 2 * t + 1, r, :]
            top = jnp.where(low_half, even, shift_lanes(odd, 64))
            bottom = jnp.where(low_half, shift_lanes(even, 64), odd)
            high, low = split(jnp.concatenate([top, bottom], axis=0))
            piece_ref[0, 16 * r : 16 * r + 16, 128 * t : 128 * t + 128] = high
            piece_ref[1, 16 * r : 16 * r + 16, 128 * t : 128 * t + 128] = low
    rho = slot_ref[2:3, :]
    own = (rho >= 0) & (rho < 8)
    lane = row_lanes(ids_ref, rows_ref, slot_ref[0:1, :])
    kind = slot_ref[1:2, :]
    row = iota((384, 512), 0)

    def spread(n):
        one_hot = jnp.where(row == jnp.where((kind == n) & own, lane, -1), 1.0, 0.0).astype(BF16)
        return (dot(piece_ref[0], one_hot, NT) + dot(piece_ref[1], one_hot, NT)).reshape(COLS, LEV, 384)

    flag = jnp.zeros((1, 384), F32)
    at = jnp.where(ids_ref[0] >= 2, FROWS, 0)
    lanes = iota((1, 384), 1)
    for k in range(FROWS):
        e = rows_ref[at + k] - BAND * ids_ref[0]
        e = jnp.where((e < 0) & (e >= -2), e + 384, e)
        flag = jnp.where(lanes == e, 1.0, flag)
    flagged = flag > 0.5
    c, qc = tab_ref[2:3, :], tab_ref[3:4, :]
    hp, dv = spread(0), spread(1)
    dv = jnp.where(flagged, dv, 0.25 * row_difference(hp))
    dp = -qc * row_difference(c * dv)

    def put(field, n, plain):
        out_ref[field] = jnp.where(flagged, spread(n)[0:SEG], plain)[:, :, 0:BAND]

    put(1, 3, next_ref[0] + dv[0:SEG])
    put(3, 5, zonal_ref[1] + dp[0:SEG])
    put(0, 2, zonal_ref[0])
    put(2, 4, next_ref[1])
    put(4, 6, next_ref[3])


VMEM = pl.BlockSpec(memory_space=pltpu.VMEM)
SMEM = pl.BlockSpec(memory_space=pltpu.SMEM)


def call(body, name, specs, args, outs, scratch, flops, mib):
    return pl.pallas_call(
        body,
        name=name,
        out_shape=outs,
        in_specs=list(specs),
        out_specs=jax.tree.map(lambda _: VMEM, outs),
        scratch_shapes=scratch,
        compiler_params=pltpu.CompilerParams(vmem_limit_bytes=mib << 20),
        cost_estimate=pl.CostEstimate(flops=flops, bytes_accessed=8 << 20, transcendentals=0),
    )(*args)


def shape(*dims):
    return jax.ShapeDtypeStruct(dims, F32)


def neighbours():
    first, second = [], []
    for l in range(64):
        for b in (0, 2):
            first += [(64 * b + l, 64 * b + 64 + l), (64 * b + 64 + l, 64 * b + l)]
        second += [(64 + l, 128 + l), (128 + l, 64 + l)]
        second += [(l, (l + 32) % 64), (192 + l, 192 + (l + 32) % 64)]
    return first, second


def exchange(edges):
    east, west, first, second = edges
    pairs_first, pairs_second = neighbours()
    got_first = lax.ppermute(first, ("lat", "lon"), pairs_first)
    got_second = lax.ppermute(second, ("lat", "lon"), pairs_second)
    from_west = lax.ppermute(east, "lon", [(i, (i + 1) % 64) for i in range(64)])
    from_east = lax.ppermute(west, "lon", [((i + 1) % 64, i) for i in range(64)])
    return from_west, from_east, got_first, got_second


def row_tables(b):
    def cosine(row):
        return jnp.abs(jnp.sin((row.astype(F32) + 0.5) * (jnp.pi / NLAT)))

    lane = jnp.arange(384, dtype=I32)
    row = jnp.where(lane < 370, lane, lane - 384) + BAND * b
    c = cosine(row)
    f = -0.2 * jnp.cos((row.astype(F32) + 0.5) * (jnp.pi / NLAT))
    polar = cosine(jnp.zeros((), I32))
    zero = jnp.zeros_like(c)
    tab = jnp.stack([0.5 * polar / c, f, c, 0.25 / c, zero, zero, zero, zero])
    return tab, cosine(jnp.arange(-1, 1447, dtype=I32))


def per_device(prognostic, filter_rows, cutoff):
    b, lon = lax.axis_index("lat"), lax.axis_index("lon")
    ids = jnp.stack([b, lon]).astype(I32)
    tab, cosines = row_tables(b)
    tab, cosines = lax.optimization_barrier((tab, cosines))
    rho64, kind64 = slot_tables()
    slots = np.full((8, 512), -1, np.int32)
    slots[0] = (8 * np.arange(8)[:, None] + rho64[None, :]).reshape(-1)
    slots[1] = np.tile(kind64, 8)
    slots[2] = np.tile(rho64, 8)
    slots[3] = np.tile(kind64, 8)
    margin = (slots[2] < 0) | (slots[2] > 7)
    slots[3] = np.where(margin & (slots[1] == 1), 0, slots[3])
    slots = jnp.asarray(slots)
    constants = [jnp.asarray(x) for x in fourier_constants()]

    start = prognostic.transpose(0, 2, 1, 3)
    edge_shapes = (shape(4, 8, 384), shape(4, 8, 384), shape(2, EDGE), shape(2, EDGE))
    edges = call(
        edges_kernel, "edges", (SMEM, VMEM), (ids, start), edge_shapes,
        [pltpu.VMEM((3, SEG, LEV, 384), F32)], 10**7, 16,
    )
    state, *edges = call(
        first_kernel, "first", (SMEM, *[VMEM] * 6), (ids, start, *exchange(edges), tab),
        (shape(5, SEG, LEV, 384), *edge_shapes),
        [pltpu.VMEM((3, 49, LEV, 384), F32), pltpu.VMEM((16, EDGE), F32), pltpu.VMEM((47, LEV, 384), F32)],
        10**8, 24,
    )
    from_west, from_east, got_first, got_second = exchange(edges)
    message, after = call(
        pack_kernel, "pack", (SMEM, SMEM, *[VMEM] * 5),
        (ids, filter_rows, state, got_first, got_second, tab, slots),
        (shape(8, 8, MROWS, 128), shape(4, SEG, LEV, 384)),
        [
            pltpu.VMEM((2, LEV * COLS, 7 * 384), BF16),
            pltpu.VMEM((16, EDGE), F32),
            pltpu.VMEM((3, SEG, LEV, 384), F32),
        ],
        10**9, 32,
    )
    zonal = call(
        zonal_kernel, "zonal", [VMEM] * 5, (state, after, from_west, from_east, tab),
        shape(2, SEG, LEV, 384),
        [pltpu.VMEM((3, 49, LEV, 384), F32), pltpu.VMEM((47, LEV, 384), F32)], 10**8, 16,
    )
    message, zonal = lax.optimization_barrier((message, zonal))
    whole = lax.all_to_all(message.reshape(64, MROWS, 128), "lon", split_axis=0, concat_axis=0, tiled=True)
    answer = call(
        spectral_kernel, "spectral", (*[SMEM] * 4, *[VMEM] * 7),
        (ids, filter_rows, cutoff, cosines, whole, slots, *constants),
        shape(64, MROWS, 128),
        [
            pltpu.VMEM((40, 48, 128), F32),
            pltpu.VMEM((PAIRS, 96, 128), F32),
            pltpu.VMEM((24, 96, 128), F32),
            pltpu.VMEM((512, 256), BF16),
        ],
        10**9, 32,
    )
    back = lax.all_to_all(answer, "lon", split_axis=0, concat_axis=0, tiled=True)
    out = call(
        final_kernel, "final", (SMEM, SMEM, *[VMEM] * 5),
        (ids, filter_rows, back.reshape(8, 8, MROWS, 128), after, zonal, tab, slots),
        shape(FIELDS, SEG, LEV, BAND),
        [pltpu.VMEM((2, LEV * COLS, 512), BF16)], 10**9, 32,
    )
    return out.transpose(0, 2, 1, 3)


def solution(mesh):
    in_specs = (P(None, None, "lon", "lat"), P(), P())
    out_specs = P(None, None, "lon", "lat")
    return jax.shard_map(
        per_device, mesh=mesh, in_specs=in_specs, out_specs=out_specs, check_vma=False
    )
```

```python
import jax
import jax.numpy as jnp
import ml_dtypes
import numpy as np
from jax import lax
from jax.experimental import pallas as pl
from jax.experimental.pallas import tpu as pltpu
from jax.sharding import PartitionSpec as P

NLON, NLAT, LEV = 2880, 1440, 8
SEG, BAND, FROWS, FIELDS = 45, 360, 64, 5
F32, BF16, I32 = jnp.float32, jnp.bfloat16, jnp.int32
NN = (((1,), (0,)), ((), ()))
NT = (((1,), (1,)), ((), ()))
TN = (((0,), (0,)), ((), ()))

SLOT_BASE = (0, 12, 22, 30, 38, 46, 54)
SLOT_COUNT = (12, 10, 8, 8, 8, 8, 8)
SLOT_FIRST = (-2, -1, 0, 0, 0, 0, 0)
PAIRS = 17
MROWS = 23
COLS = 2 * MROWS
EDGE = 3 * SEG * LEV


def slot_tables():
    rho = np.full(64, -100, np.int32)
    kind = np.full(64, -1, np.int32)
    for f, (base, count, first) in enumerate(zip(SLOT_BASE, SLOT_COUNT, SLOT_FIRST)):
        rho[base : base + count] = first + np.arange(count)
        kind[base : base + count] = f
    return rho, kind


def split_np(m):
    high = m.astype(ml_dtypes.bfloat16)
    low = (m - high.astype(np.float64)).astype(ml_dtypes.bfloat16)
    return high, low


def triple(m):
    high, low = split_np(m)
    return np.concatenate([high, low, high], axis=-1)


def fourier_constants():
    s = np.arange(64)
    k1 = np.arange(33)
    ang = 2 * np.pi * (np.outer(k1, s) % 64) / 64
    fwd = np.zeros((80, 64))
    fwd[:33], fwd[40:73] = np.cos(ang), -np.sin(ang)
    inv = np.zeros((2, 64, 2, 24))
    sig = np.zeros((PAIRS, 96, 128))
    mf = np.zeros((2 * PAIRS, 192, 48))
    mi = np.zeros((PAIRS, 192, 96))
    i, k2 = np.arange(SEG), np.arange(SEG)
    for q in range(33):
        half, pair = divmod(q, PAIRS)
        inv[half, :, 0, pair] = np.cos(ang[q])
        inv[half, :, 1, pair] = -np.sin(ang[q])
        k = q + 64 * k2
        w = 2 * np.pi * (np.outer(k, i) % NLON) / NLON
        full = np.zeros((2, 48, 2, 48))
        full[0, :SEG, 0, :SEG], full[0, :SEG, 1, :SEG] = np.cos(w), np.sin(w)
        full[1, :SEG, 0, :SEG], full[1, :SEG, 1, :SEG] = -np.sin(w), np.cos(w)
        for h in range(2):
            mf[q, 96 * h : 96 * h + 96] = np.stack([np.pad(full[:, :, n, h : 2 * MROWS : 2], ((0, 0), (0, 0), (0, 1))) for n in range(2)], axis=2).reshape(96, 48)
        scale = (1.0 if q in (0, 32) else 2.0) / NLON
        mi[pair, 96 * half : 96 * half + 96] = full.reshape(96, 96).T * scale
        sn = np.sin(2 * np.pi * k / NLON)
        sig[pair, :SEG, 64 * half : 64 * half + 64] = -sn[:, None]
        sig[pair, 48 : 48 + SEG, 64 * half : 64 * half + 64] = sn[:, None]
    return (
        triple(fwd),
        triple(inv.reshape(128, 48)),
        np.concatenate(split_np(mf), axis=-1),
        np.concatenate(split_np(mi), axis=-1),
        sig.astype(np.float32),
    )


def dot(a, b, dims=NN):
    return lax.dot_general(a, b, dims, preferred_element_type=F32)


def split(x):
    high = x.astype(BF16)
    return high, (x - high.astype(F32)).astype(BF16)


def iota(shape, axis):
    return lax.broadcasted_iota(I32, shape, axis)


def edge_rows(fields, even):
    r, lane = iota((16, 384), 0), iota((16, 384), 1)
    north = (r < 2) == even
    target = jnp.where(north, BAND - 1 - r % 2, r % 2)
    pick = jnp.where((lane == target) & (r < 4), 1.0, 0.0).astype(BF16)
    high, low = split(fields)
    return dot(pick, high, NT) + dot(pick, low, NT)


def placed_rows(first_ref, second_ref, rows_ref, even, polar):
    rows_ref[...] = jnp.zeros_like(rows_ref)
    rows_ref[0:2, :] = first_ref[...]
    wind = iota((2, EDGE), 1) < 720
    second = second_ref[...]
    rows_ref[2:4, :] = jnp.where(wind & polar, -second, second)
    r, lane = iota((16, 384), 0), iota((16, 384), 1)
    north = (r < 2) == even
    target = jnp.where(north, BAND + r % 2, 383 - r % 2)
    put = jnp.where((lane == target) & (r < 4), 1.0, 0.0).astype(BF16)
    high, low = split(rows_ref[...])
    return (dot(high, put, TN) + dot(low, put, TN)).reshape(3, SEG, LEV, 384)


def lat_of(ids_ref):
    b = ids_ref[0]
    return b, b % 2 == 0, (b == 0) | (b == 3)


def shift_lanes(x, by):
    return pltpu.roll(x, by % x.shape[-1], x.ndim - 1)


def level_difference(x):
    lev = iota(x.shape, x.ndim - 2)
    above = jnp.where(lev < LEV - 1, pltpu.roll(x, LEV - 1, x.ndim - 2), 0.0)
    below = jnp.where(lev > 0, pltpu.roll(x, 1, x.ndim - 2), 0.0)
    return above - below


def row_difference(x):
    return shift_lanes(x, -1) - shift_lanes(x, 1)


def edges_kernel(ids_ref, state_ref, east_ref, west_ref, first_ref, second_ref, box_ref):
    _, even, _ = lat_of(ids_ref)
    box_ref[:, :, :, 256:384] = jnp.zeros((3, SEG, LEV, 128), F32)
    for n, field in enumerate((0, 1, 3)):
        box_ref[n, :, :, 0:BAND] = state_ref[field]
    send_edges(box_ref, (0, 1, 2), even, east_ref, west_ref, first_ref, second_ref)


def send_edges(box_ref, uvp, even, east_ref, west_ref, first_ref, second_ref):
    u, v, p = uvp
    for slot, (f, e, w) in enumerate(((p, 43, 1), (p, 44, 0), (u, 44, 0), (v, 44, 0))):
        east_ref[slot] = box_ref[f, e]
        west_ref[slot] = box_ref[f, w]
    fields = jnp.concatenate([box_ref[f].reshape(360, 384) for f in uvp], axis=0)
    rows = edge_rows(fields, even)
    first_ref[...] = rows[0:2]
    second_ref[...] = rows[2:4]


def fill_columns(ext_ref, from_west_ref, from_east_ref):
    for slot, (f, west, east) in enumerate(((2, 0, 48), (2, 1, 47), (0, 1, 47), (1, 1, 47))):
        ext_ref[f, west] = from_west_ref[slot]
        ext_ref[f, east] = from_east_ref[slot]


CHUNKS = tuple((i, min(i + 5, SEG)) for i in range(0, SEG, 5))


def first_kernel(
    ids_ref, state_ref, from_west_ref, from_east_ref, got_first_ref, got_second_ref, tab_ref,
    out_ref, east_ref, west_ref, first_ref, second_ref, ext_ref, rows_ref, new_u_ref,
):
    _, even, polar = lat_of(ids_ref)
    ext_ref[:, 2:47] = placed_rows(got_first_ref, got_second_ref, rows_ref, even, polar)
    for n, field in enumerate((0, 1, 3)):
        ext_ref[n, 2:47, :, 0:BAND] = state_ref[field]
    fill_columns(ext_ref, from_west_ref, from_east_ref)
    a, f, c, qc = (tab_ref[n : n + 1, :] for n in range(4))
    out_ref[:, :, :, 256:384] = jnp.zeros((5, SEG, LEV, 128), F32)
    for i, end in ((-1, 0), *CHUNKS, (45, 46)):
        new_u_ref[i + 1 : end + 1] = (
            ext_ref[0, i + 2 : end + 2]
            - (0.5 * a) * (ext_ref[2, i + 3 : end + 3] - ext_ref[2, i + 1 : end + 1])
            + f * ext_ref[1, i + 2 : end + 2]
        )
    for i, end in CHUNKS:
        at = slice(i + 2, end + 2)
        p = ext_ref[2, at]
        new_v = ext_ref[1, at] - 0.25 * row_difference(p) - f * ext_ref[0, at]
        new_p = p - (0.5 * a) * (new_u_ref[i + 2 : end + 2] - new_u_ref[i:end])
        new_p -= qc * row_difference(c * new_v)
        th = state_ref[4, i:end]
        new_w = state_ref[2, i:end] - 0.25 * level_difference(state_ref[3, i:end]) + 0.3 * th
        out_ref[0, i:end, :, 0:BAND] = new_u_ref[i + 1 : end + 1, :, 0:BAND]
        out_ref[1, i:end, :, 0:BAND] = new_v[:, :, 0:BAND]
        out_ref[2, i:end, :, 0:BAND] = new_w
        out_ref[3, i:end, :, 0:BAND] = new_p[:, :, 0:BAND] - 0.25 * level_difference(new_w)
        out_ref[4, i:end, :, 0:BAND] = th - 0.3 * new_w
    send_edges(out_ref, (0, 1, 3), even, east_ref, west_ref, first_ref, second_ref)


def row_lanes(ids_ref, rows_ref, index):
    b = ids_ref[0]
    at = jnp.where(b >= 2, FROWS, 0)
    lane = jnp.full(index.shape, -1, I32)
    for k in range(FROWS):
        e = rows_ref[at + k] - BAND * b
        e = jnp.where(e < 0, jnp.where(e >= -2, e + 384, -1), jnp.where(e <= BAND + 1, e, -1))
        lane = jnp.where(index == k, e, lane)
    return lane


def pack_kernel(
    ids_ref, rows_ref, r_ref, got_first_ref, got_second_ref, tab_ref, slot_ref,
    out_ref, next_ref, hot_ref, x_ref, edge_ref, placed_ref,
):
    _, even, polar = lat_of(ids_ref)
    placed_ref[...] = placed_rows(got_first_ref, got_second_ref, edge_ref, even, polar)
    a, f, c, qc = (tab_ref[n : n + 1, :] for n in range(4))
    for i in range(0, SEG, 6):
        end = min(i + 6, SEG)
        at = slice(i, end)
        u = r_ref[0, at] + placed_ref[0, at]
        v = r_ref[1, at] + placed_ref[1, at]
        p = r_ref[3, at] + placed_ref[2, at]
        th = r_ref[4, at]
        g = v - f * u
        new_v = g - 0.25 * row_difference(p)
        new_w = r_ref[2, at] - 0.25 * level_difference(p) + 0.3 * th
        new_p = p - qc * row_difference(c * new_v) - 0.25 * level_difference(new_w)
        new_t = th - 0.3 * new_w
        for n, value in enumerate((new_v, new_w, new_p, new_t)):
            next_ref[n, at] = value
        rows = slice(LEV * i, LEV * (end + (end - i) % 2))
        for n, value in enumerate((p, g, u + f * v, new_v, new_w, new_p, new_t)):
            if (end - i) % 2:
                value = jnp.concatenate([value, jnp.zeros((1, LEV, 384), F32)], axis=0)
            high, low = split(value.reshape(-1, 384))
            x_ref[0, rows, 384 * n : 384 * n + 384] = high
            x_ref[1, rows, 384 * n : 384 * n + 384] = low
    lane = row_lanes(ids_ref, rows_ref, slot_ref[0:1, :])
    kind = slot_ref[1:2, :]
    row = iota((384, 512), 0)
    for n in range(7):
        hot_ref[384 * n : 384 * n + 384] = jnp.where(row == jnp.where(kind == n, lane, -1), 1.0, 0.0).astype(BF16)
    got = dot(x_ref[0], hot_ref[...]) + dot(x_ref[1], hot_ref[...])
    low_half = iota((8, 128), 1) < 64
    for r in range(MROWS):
        for t in range(4):
            top = got[16 * r : 16 * r + 8, 128 * t : 128 * t + 128]
            bottom = got[16 * r + 8 : 16 * r + 16, 128 * t : 128 * t + 128]
            out_ref[:, 2 * t, r, :] = jnp.where(low_half, top, shift_lanes(bottom, 64))
            out_ref[:, 2 * t + 1, r, :] = jnp.where(low_half, shift_lanes(top, 64), bottom)


def zonal_kernel(r_ref, p2_ref, from_west_ref, from_east_ref, tab_ref, out_ref, ext_ref, new_u_ref):
    a, f = tab_ref[0:1, :], tab_ref[1:2, :]
    for n, field in enumerate((0, 1, 3)):
        ext_ref[n, 2:47] = r_ref[field]
    fill_columns(ext_ref, from_west_ref, from_east_ref)
    for i, end in ((-1, 0), *CHUNKS, (45, 46)):
        new_u_ref[i + 1 : end + 1] = (
            ext_ref[0, i + 2 : end + 2]
            - (0.5 * a) * (ext_ref[2, i + 3 : end + 3] - ext_ref[2, i + 1 : end + 1])
            + f * ext_ref[1, i + 2 : end + 2]
        )
    for i, end in CHUNKS:
        out_ref[0, i:end] = new_u_ref[i + 1 : end + 1]
        out_ref[1, i:end] = p2_ref[2, i:end] - (0.5 * a) * (new_u_ref[i + 2 : end + 2] - new_u_ref[i:end])


def spectral_kernel(
    ids_ref, rows_ref, cut_ref, cos_ref, in_ref, slot_ref, fwd_ref, inv_ref, mf_ref, mi_ref, sig_ref,
    out_ref, z_ref, s_ref, y_ref, mix_ref,
):
    b, owner = ids_ref[0], ids_ref[1]
    at = jnp.where(b >= 2, FROWS, 0)
    first = 8 * (owner % 8)
    low_half = iota((96, 128), 1) < 64

    rho = slot_ref[2:3, 0:128]
    kind = slot_ref[3:4, 0:128]

    def listed(k):
        return jnp.where((k >= 0) & (k < FROWS), rows_ref[at + jnp.clip(k, 0, FROWS - 1)], -1000)

    row_at = [listed(first + t) for t in range(-4, 12)]
    cut_at = [cut_ref[at + jnp.clip(first + t, 0, FROWS - 1)] for t in range(-4, 12)]
    blank = jnp.zeros((1, 128), F32)
    rows = [jnp.full((1, 128), -1000, I32) for _ in range(5)]
    cut, c0, cp, cm = jnp.zeros((1, 128), I32), blank + 1.0, blank, blank
    for t in range(-2, 10):
        here = rho == t
        jc = jnp.clip(row_at[t + 4], 0, NLAT - 1)
        for d in range(-2, 3):
            rows[d + 2] = jnp.where(here, row_at[t + d + 4], rows[d + 2])
        cut = jnp.where(here, cut_at[t + 4], cut)
        cm = jnp.where(here, cos_ref[jc], cm)
        c0 = jnp.where(here, cos_ref[jc + 1], c0)
        cp = jnp.where(here, cos_ref[jc + 2], cp)
    j = rows[2]

    def yes(cond):
        return jnp.where(cond, 1.0, 0.0)

    up1, dn1 = yes(rows[3] == j + 1), yes(rows[1] == j - 1)
    up2, up22 = yes(rows[3] == j + 2), yes(rows[4] == j + 2)
    dn2, dn22 = yes(rows[1] == j - 2), yes(rows[0] == j - 2)
    south, north = yes(j == 0), yes(j == NLAT - 1)
    a = 0.5 * cos_ref[1] / c0
    qc = -0.25 / c0
    src, dst = iota((128, 128), 0), iota((128, 128), 1)

    def mix(n, terms):
        total = jnp.zeros((128, 128), F32)
        for to, shift, coef in terms:
            total += jnp.where(src == dst - shift, jnp.where(kind == to, coef, 0.0), 0.0)
        high, low = split(total)
        mix_ref[128 * n : 128 * n + 128, 0:128] = high
        mix_ref[128 * n : 128 * n + 128, 128:256] = low

    q0 = -0.25 * (cp * (1 - north) + cm * (1 - south) + c0 * (south + north))
    pole = 0.25 * (north - south)
    mix(0, [(2, 20, -a), (5, 24, -a)])
    mix(1, [(5, 44, -a * a)])
    mix(
        2,
        [
            (1, 10, 0.25 * up1), (1, 12, -0.25 * dn1),
            (3, 27, 0.25 * up1), (3, 29, -0.25 * dn1), (3, 17, blank - 1.0),
            (5, 44, qc * q0),
            (5, 43, qc * 0.25 * cp * up2), (5, 42, qc * 0.25 * cp * up22),
            (5, 45, qc * 0.25 * cm * dn2), (5, 46, qc * 0.25 * cm * dn22),
            (5, 32, -qc * cp * up1), (5, 34, qc * cm * dn1),
        ],
    )
    mix(
        3,
        [
            (1, 11, pole), (3, 28, pole),
            (5, 43, qc * 0.25 * (cp * yes(j == NLAT - 2) + c0 * south * up1)),
            (5, 45, qc * 0.25 * (cm * yes(j == 1) + c0 * north * dn1)),
            (5, 33, qc * c0 * (north - south)),
        ],
    )

    z_ref[:, MROWS, :] = jnp.zeros((40, 128), F32)
    z_ref[:, 24 + MROWS, :] = jnp.zeros((40, 128), F32)
    for r in range(0, MROWS, 2):
        pieces = []
        for q in range(r, min(r + 2, MROWS)):
            high, low = split(in_ref[:, q, :])
            pieces.append(jnp.concatenate([high, high, low], axis=0))
        z = dot(fwd_ref[...], pieces[0] if len(pieces) == 1 else jnp.concatenate(pieces, axis=1))
        for n in range(len(pieces)):
            z_ref[:, r + n, :] = z[0:40, 128 * n : 128 * n + 128]
            z_ref[:, 24 + r + n, :] = z[40:80, 128 * n : 128 * n + 128]

    def both_pieces(x):
        high, low = split(x)
        return jnp.concatenate(
            [jnp.concatenate([high, low], axis=1), jnp.concatenate([high, jnp.zeros_like(low)], axis=1)], axis=0
        )

    for pair in range(PAIRS):
        parts = []
        for half in range(2):
            got = dot(mf_ref[pair + PAIRS * half], both_pieces(z_ref[pair + PAIRS * half]))
            parts.append(got[:, 0:128] + got[:, 128:256])
        s_ref[pair] = jnp.where(
            low_half,
            parts[0][0:96] + shift_lanes(parts[0][96:192], 64),
            shift_lanes(parts[1][0:96], 64) + parts[1][96:192],
        )
    final = kind >= 2
    sign = jnp.where(kind == 1, -1.0, 1.0)
    k_base = 64 * (iota((96, 128), 0) % 48) + jnp.where(low_half, 0, PAIRS)
    odd_base = jnp.where(low_half, 1.0, -1.0)
    for pair in range(PAIRS):
        s = s_ref[pair]
        k = k_base + pair
        keep = jnp.minimum(k, NLON - k) <= cut
        h = jnp.where(keep, 0.0, s)
        sig = sig_ref[pair]
        d = sig * jnp.concatenate([s[48:96], s[0:48]], axis=0)
        ph = (odd_base if pair % 2 == 0 else -odd_base) * h
        high, low = split(jnp.concatenate([d, sig * sig * s, h, ph], axis=1))
        corr = dot(high, mix_ref[...])
        corr = corr[:, 0:128] + corr[:, 128:256] + dot(low, mix_ref[:, 0:128])
        s_ref[pair] = jnp.where(final, jnp.where(keep, s + corr, 0.0), sign * h + corr)
    y_ref[PAIRS:24] = jnp.zeros((24 - PAIRS, 96, 128), F32)
    for pair in range(PAIRS):
        back = dot(mi_ref[pair], both_pieces(s_ref[pair]))
        back = back[:, 0:128] + back[:, 128:256]
        y_ref[pair] = jnp.where(low_half, back[0:96], back[96:192])
    half64 = iota((64, 128), 1) < 64
    for r in range(MROWS):
        cols = []
        for i in (2 * r, 2 * r + 1):
            zz = jnp.concatenate([y_ref[:, i, :], y_ref[:, 48 + i, :]], axis=0)
            high, low = split(zz)
            cols.append(jnp.concatenate([high, high, low], axis=0))
        x = dot(inv_ref[...], jnp.concatenate(cols, axis=1))
        out_ref[:, r, :] = jnp.where(
            half64,
            x[0:64, 0:128] + shift_lanes(x[64:128, 0:128], 64),
            shift_lanes(x[0:64, 128:256], 64) + x[64:128, 128:256],
        )


def final_kernel(ids_ref, rows_ref, in_ref, next_ref, zonal_ref, tab_ref, slot_ref, hot_ref, out_ref, piece_ref, done_ref, sems):
    low_half = iota((8, 128), 1) < 64
    for r in range(MROWS):
        for t in range(4):
            even, odd = in_ref[:, 2 * t, r, :], in_ref[:, 2 * t + 1, r, :]
            top = jnp.where(low_half, even, shift_lanes(odd, 64))
            bottom = jnp.where(low_half, shift_lanes(even, 64), odd)
            high, low = split(jnp.concatenate([top, bottom], axis=0))
            piece_ref[0, 16 * r : 16 * r + 16, 128 * t : 128 * t + 128] = high
            piece_ref[1, 16 * r : 16 * r + 16, 128 * t : 128 * t + 128] = low
    rho = slot_ref[2:3, :]
    own = jnp.where((rho >= 0) & (rho < 8), 1.0, 0.0).astype(BF16)

    def spread(n):
        one_hot = hot_ref[384 * n : 384 * n + 384]
        if n < 2:
            one_hot = one_hot * own
        return (dot(piece_ref[0], one_hot, NT) + dot(piece_ref[1], one_hot, NT)).reshape(COLS, LEV, 384)

    flag = jnp.zeros((1, 384), F32)
    at = jnp.where(ids_ref[0] >= 2, FROWS, 0)
    lanes = iota((1, 384), 1)
    for k in range(FROWS):
        e = rows_ref[at + k] - BAND * ids_ref[0]
        e = jnp.where((e < 0) & (e >= -2), e + 384, e)
        flag = jnp.where(lanes == e, 1.0, flag)
    flagged = flag > 0.5
    c, qc = tab_ref[2:3, :], tab_ref[3:4, :]
    hp, dv = spread(0), spread(1)
    dv = jnp.where(flagged, dv, 0.25 * row_difference(hp))
    dp = -qc * row_difference(c * dv)

    stores = []

    def put(field, n, plain):
        done_ref[field] = jnp.where(flagged, spread(n)[0:SEG], plain)[:, :, 0:BAND]
        stores.append(pltpu.make_async_copy(done_ref.at[field], out_ref.at[field], sems.at[field]))
        stores[-1].start()

    put(1, 3, next_ref[0] + dv[0:SEG])
    put(3, 5, zonal_ref[1] + dp[0:SEG])
    put(0, 2, zonal_ref[0])
    put(2, 4, next_ref[1])
    put(4, 6, next_ref[3])
    for store in stores:
        store.wait()


VMEM = pl.BlockSpec(memory_space=pltpu.VMEM)
SMEM = pl.BlockSpec(memory_space=pltpu.SMEM)
ANY = pl.BlockSpec(memory_space=pl.ANY)


def call(body, name, specs, args, outs, scratch, flops, mib, out_spec=None):
    return pl.pallas_call(
        body,
        name=name,
        out_shape=outs,
        in_specs=list(specs),
        out_specs=jax.tree.map(lambda _: out_spec or VMEM, outs),
        scratch_shapes=scratch,
        compiler_params=pltpu.CompilerParams(vmem_limit_bytes=mib << 20),
        cost_estimate=pl.CostEstimate(flops=flops, bytes_accessed=8 << 20, transcendentals=0),
    )(*args)


def shape(*dims):
    return jax.ShapeDtypeStruct(dims, F32)


def neighbours():
    first, second = [], []
    for l in range(64):
        for b in (0, 2):
            first += [(64 * b + l, 64 * b + 64 + l), (64 * b + 64 + l, 64 * b + l)]
        second += [(64 + l, 128 + l), (128 + l, 64 + l)]
        second += [(l, (l + 32) % 64), (192 + l, 192 + (l + 32) % 64)]
    return first, second


def exchange(edges):
    east, west, first, second = edges
    pairs_first, pairs_second = neighbours()
    got_first = lax.ppermute(first, ("lat", "lon"), pairs_first)
    got_second = lax.ppermute(second, ("lat", "lon"), pairs_second)
    from_west = lax.ppermute(east, "lon", [(i, (i + 1) % 64) for i in range(64)])
    from_east = lax.ppermute(west, "lon", [((i + 1) % 64, i) for i in range(64)])
    return from_west, from_east, got_first, got_second


def row_tables(b):
    def cosine(row):
        return jnp.abs(jnp.sin((row.astype(F32) + 0.5) * (jnp.pi / NLAT)))

    lane = jnp.arange(384, dtype=I32)
    row = jnp.where(lane < 370, lane, lane - 384) + BAND * b
    c = cosine(row)
    f = -0.2 * jnp.cos((row.astype(F32) + 0.5) * (jnp.pi / NLAT))
    polar = cosine(jnp.zeros((), I32))
    zero = jnp.zeros_like(c)
    tab = jnp.stack([0.5 * polar / c, f, c, 0.25 / c, zero, zero, zero, zero])
    return tab, cosine(jnp.arange(-1, 1447, dtype=I32))


def per_device(prognostic, filter_rows, cutoff):
    b, lon = lax.axis_index("lat"), lax.axis_index("lon")
    ids = jnp.stack([b, lon]).astype(I32)
    tab, cosines = row_tables(b)
    tab, cosines = lax.optimization_barrier((tab, cosines))
    rho64, kind64 = slot_tables()
    slots = np.full((8, 512), -1, np.int32)
    slots[0] = (8 * np.arange(8)[:, None] + rho64[None, :]).reshape(-1)
    slots[1] = np.tile(kind64, 8)
    slots[2] = np.tile(rho64, 8)
    slots[3] = np.tile(kind64, 8)
    margin = (slots[2] < 0) | (slots[2] > 7)
    slots[3] = np.where(margin & (slots[1] == 1), 0, slots[3])
    slots = jnp.asarray(slots)
    constants = [jnp.asarray(x) for x in fourier_constants()]

    start = prognostic.transpose(0, 2, 1, 3)
    edge_shapes = (shape(4, 8, 384), shape(4, 8, 384), shape(2, EDGE), shape(2, EDGE))
    edges = call(
        edges_kernel, "edges", (SMEM, VMEM), (ids, start), edge_shapes,
        [pltpu.VMEM((3, SEG, LEV, 384), F32)], 10**7, 16,
    )
    state, *edges = call(
        first_kernel, "first", (SMEM, *[VMEM] * 6), (ids, start, *exchange(edges), tab),
        (shape(5, SEG, LEV, 384), *edge_shapes),
        [pltpu.VMEM((3, 49, LEV, 384), F32), pltpu.VMEM((16, EDGE), F32), pltpu.VMEM((47, LEV, 384), F32)],
        10**8, 24,
    )
    from_west, from_east, got_first, got_second = exchange(edges)
    message, after, hot = call(
        pack_kernel, "pack", (SMEM, SMEM, *[VMEM] * 5),
        (ids, filter_rows, state, got_first, got_second, tab, slots),
        (shape(8, 8, MROWS, 128), shape(4, SEG, LEV, 384), jax.ShapeDtypeStruct((7 * 384, 512), BF16)),
        [
            pltpu.VMEM((2, LEV * COLS, 7 * 384), BF16),
            pltpu.VMEM((16, EDGE), F32),
            pltpu.VMEM((3, SEG, LEV, 384), F32),
        ],
        10**9, 32,
    )
    zonal = call(
        zonal_kernel, "zonal", [VMEM] * 5, (state, after, from_west, from_east, tab),
        shape(2, SEG, LEV, 384),
        [pltpu.VMEM((3, 49, LEV, 384), F32), pltpu.VMEM((47, LEV, 384), F32)], 10**8, 16,
    )
    message, zonal = lax.optimization_barrier((message, zonal))
    whole = lax.all_to_all(message.reshape(64, MROWS, 128), "lon", split_axis=0, concat_axis=0, tiled=True)
    answer = call(
        spectral_kernel, "spectral", (*[SMEM] * 4, *[VMEM] * 7),
        (ids, filter_rows, cutoff, cosines, whole, slots, *constants),
        shape(64, MROWS, 128),
        [
            pltpu.VMEM((40, 48, 128), F32),
            pltpu.VMEM((PAIRS, 96, 128), F32),
            pltpu.VMEM((24, 96, 128), F32),
            pltpu.VMEM((512, 256), BF16),
        ],
        10**9, 32,
    )
    back = lax.all_to_all(answer, "lon", split_axis=0, concat_axis=0, tiled=True)
    out = call(
        final_kernel, "final", (SMEM, SMEM, *[VMEM] * 6),
        (ids, filter_rows, back.reshape(8, 8, MROWS, 128), after, zonal, tab, slots, hot),
        shape(FIELDS, SEG, LEV, BAND),
        [
            pltpu.VMEM((2, LEV * COLS, 512), BF16),
            pltpu.VMEM((FIELDS, SEG, LEV, BAND), F32),
            pltpu.SemaphoreType.DMA((FIELDS,)),
        ],
        10**9, 32, ANY,
    )
    return out.transpose(0, 2, 1, 3)


def solution(mesh):
    in_specs = (P(None, None, "lon", "lat"), P(), P())
    out_specs = P(None, None, "lon", "lat")
    return jax.shard_map(
        per_device, mesh=mesh, in_specs=in_specs, out_specs=out_specs, check_vma=False
    )
```

```python
import jax
import jax.numpy as jnp
import ml_dtypes
import numpy as np
from jax import lax
from jax.experimental import pallas as pl
from jax.experimental.pallas import tpu as pltpu
from jax.sharding import PartitionSpec as P

NLON, NLAT, LEV = 2880, 1440, 8
SEG, BAND, FROWS, FIELDS = 45, 360, 64, 5
F32, BF16, I32 = jnp.float32, jnp.bfloat16, jnp.int32
NN = (((1,), (0,)), ((), ()))
NT = (((1,), (1,)), ((), ()))
TN = (((0,), (0,)), ((), ()))

SLOT_BASE = (0, 12, 22, 30, 38, 46, 54)
SLOT_COUNT = (12, 10, 8, 8, 8, 8, 8)
SLOT_FIRST = (-2, -1, 0, 0, 0, 0, 0)
PAIRS = 17
MROWS = 23
COLS = 2 * MROWS
EDGE = 3 * SEG * LEV


def slot_tables():
    rho = np.full(64, -100, np.int32)
    kind = np.full(64, -1, np.int32)
    for f, (base, count, first) in enumerate(zip(SLOT_BASE, SLOT_COUNT, SLOT_FIRST)):
        rho[base : base + count] = first + np.arange(count)
        kind[base : base + count] = f
    return rho, kind


def split_np(m):
    high = m.astype(ml_dtypes.bfloat16)
    low = (m - high.astype(np.float64)).astype(ml_dtypes.bfloat16)
    return high, low


def triple(m):
    high, low = split_np(m)
    return np.concatenate([high, low, high], axis=-1)


def fourier_constants():
    s = np.arange(64)
    k1 = np.arange(33)
    ang = 2 * np.pi * (np.outer(k1, s) % 64) / 64
    fwd = np.zeros((80, 64))
    fwd[:33], fwd[40:73] = np.cos(ang), -np.sin(ang)
    inv = np.zeros((2, 64, 2, 24))
    sig = np.zeros((PAIRS, 96, 128))
    mf = np.zeros((2 * PAIRS, 192, 48))
    mi = np.zeros((PAIRS, 192, 96))
    i, k2 = np.arange(SEG), np.arange(SEG)
    for q in range(33):
        half, pair = divmod(q, PAIRS)
        inv[half, :, 0, pair] = np.cos(ang[q])
        inv[half, :, 1, pair] = -np.sin(ang[q])
        k = q + 64 * k2
        w = 2 * np.pi * (np.outer(k, i) % NLON) / NLON
        full = np.zeros((2, 48, 2, 48))
        full[0, :SEG, 0, :SEG], full[0, :SEG, 1, :SEG] = np.cos(w), np.sin(w)
        full[1, :SEG, 0, :SEG], full[1, :SEG, 1, :SEG] = -np.sin(w), np.cos(w)
        for h in range(2):
            mf[q, 96 * h : 96 * h + 96] = np.stack([np.pad(full[:, :, n, h : 2 * MROWS : 2], ((0, 0), (0, 0), (0, 1))) for n in range(2)], axis=2).reshape(96, 48)
        scale = (1.0 if q in (0, 32) else 2.0) / NLON
        mi[pair, 96 * half : 96 * half + 96] = full.reshape(96, 96).T * scale
        sn = np.sin(2 * np.pi * k / NLON)
        sig[pair, :SEG, 64 * half : 64 * half + 64] = -sn[:, None]
        sig[pair, 48 : 48 + SEG, 64 * half : 64 * half + 64] = sn[:, None]
    return (
        triple(fwd),
        triple(inv.reshape(128, 48)),
        np.concatenate(split_np(mf), axis=-1),
        np.concatenate(split_np(mi), axis=-1),
        sig.astype(np.float32),
    )


def dot(a, b, dims=NN):
    return lax.dot_general(a, b, dims, preferred_element_type=F32)


def split(x):
    high = x.astype(BF16)
    return high, (x - high.astype(F32)).astype(BF16)


def iota(shape, axis):
    return lax.broadcasted_iota(I32, shape, axis)


def edge_rows(fields, even):
    r, lane = iota((16, 384), 0), iota((16, 384), 1)
    north = (r < 2) == even
    target = jnp.where(north, BAND - 1 - r % 2, r % 2)
    pick = jnp.where((lane == target) & (r < 4), 1.0, 0.0).astype(BF16)
    high, low = split(fields)
    return dot(pick, high, NT) + dot(pick, low, NT)


def placed_rows(first_ref, second_ref, rows_ref, even, polar):
    rows_ref[...] = jnp.zeros_like(rows_ref)
    rows_ref[0:2, :] = first_ref[...]
    wind = iota((2, EDGE), 1) < 720
    second = second_ref[...]
    rows_ref[2:4, :] = jnp.where(wind & polar, -second, second)
    r, lane = iota((16, 384), 0), iota((16, 384), 1)
    north = (r < 2) == even
    target = jnp.where(north, BAND + r % 2, 383 - r % 2)
    put = jnp.where((lane == target) & (r < 4), 1.0, 0.0).astype(BF16)
    high, low = split(rows_ref[...])
    return (dot(high, put, TN) + dot(low, put, TN)).reshape(3, SEG, LEV, 384)


def lat_of(ids_ref):
    b = ids_ref[0]
    return b, b % 2 == 0, (b == 0) | (b == 3)


def shift_lanes(x, by):
    return pltpu.roll(x, by % x.shape[-1], x.ndim - 1)


def level_difference(x):
    lev = iota(x.shape, x.ndim - 2)
    above = jnp.where(lev < LEV - 1, pltpu.roll(x, LEV - 1, x.ndim - 2), 0.0)
    below = jnp.where(lev > 0, pltpu.roll(x, 1, x.ndim - 2), 0.0)
    return above - below


def row_difference(x):
    return shift_lanes(x, -1) - shift_lanes(x, 1)


def edges_kernel(ids_ref, state_ref, east_ref, west_ref, first_ref, second_ref, box_ref):
    _, even, _ = lat_of(ids_ref)
    box_ref[:, :, :, 256:384] = jnp.zeros((3, SEG, LEV, 128), F32)
    for n, field in enumerate((0, 1, 3)):
        box_ref[n, :, :, 0:BAND] = state_ref[field]
    send_edges(box_ref, (0, 1, 2), even, east_ref, west_ref, first_ref, second_ref)


def send_edges(box_ref, uvp, even, east_ref, west_ref, first_ref, second_ref):
    u, v, p = uvp
    for slot, (f, e, w) in enumerate(((p, 43, 1), (p, 44, 0), (u, 44, 0), (v, 44, 0))):
        east_ref[slot] = box_ref[f, e]
        west_ref[slot] = box_ref[f, w]
    fields = jnp.concatenate([box_ref[f].reshape(360, 384) for f in uvp], axis=0)
    rows = edge_rows(fields, even)
    first_ref[...] = rows[0:2]
    second_ref[...] = rows[2:4]


def fill_columns(ext_ref, from_west_ref, from_east_ref):
    for slot, (f, west, east) in enumerate(((2, 0, 48), (2, 1, 47), (0, 1, 47), (1, 1, 47))):
        ext_ref[f, west] = from_west_ref[slot]
        ext_ref[f, east] = from_east_ref[slot]


CHUNKS = tuple((i, min(i + 2, SEG)) for i in range(0, SEG, 2))


def first_kernel(
    ids_ref, state_ref, from_west_ref, from_east_ref, got_first_ref, got_second_ref, tab_ref,
    out_ref, east_ref, west_ref, first_ref, second_ref, ext_ref, rows_ref, new_u_ref,
):
    _, even, polar = lat_of(ids_ref)
    ext_ref[:, 2:47] = placed_rows(got_first_ref, got_second_ref, rows_ref, even, polar)
    for n, field in enumerate((0, 1, 3)):
        ext_ref[n, 2:47, :, 0:BAND] = state_ref[field]
    fill_columns(ext_ref, from_west_ref, from_east_ref)
    a, f, c, qc = (tab_ref[n : n + 1, :] for n in range(4))
    out_ref[:, :, :, 256:384] = jnp.zeros((5, SEG, LEV, 128), F32)
    for i, end in ((-1, 0), *CHUNKS, (45, 46)):
        new_u_ref[i + 1 : end + 1] = (
            ext_ref[0, i + 2 : end + 2]
            - (0.5 * a) * (ext_ref[2, i + 3 : end + 3] - ext_ref[2, i + 1 : end + 1])
            + f * ext_ref[1, i + 2 : end + 2]
        )
    for i, end in CHUNKS:
        at = slice(i + 2, end + 2)
        p = ext_ref[2, at]
        new_v = ext_ref[1, at] - 0.25 * row_difference(p) - f * ext_ref[0, at]
        new_p = p - (0.5 * a) * (new_u_ref[i + 2 : end + 2] - new_u_ref[i:end])
        new_p -= qc * row_difference(c * new_v)
        th = state_ref[4, i:end]
        new_w = state_ref[2, i:end] - 0.25 * level_difference(state_ref[3, i:end]) + 0.3 * th
        out_ref[0, i:end, :, 0:BAND] = new_u_ref[i + 1 : end + 1, :, 0:BAND]
        out_ref[1, i:end, :, 0:BAND] = new_v[:, :, 0:BAND]
        out_ref[2, i:end, :, 0:BAND] = new_w
        out_ref[3, i:end, :, 0:BAND] = new_p[:, :, 0:BAND] - 0.25 * level_difference(new_w)
        out_ref[4, i:end, :, 0:BAND] = th - 0.3 * new_w
    send_edges(out_ref, (0, 1, 3), even, east_ref, west_ref, first_ref, second_ref)


def row_lanes(ids_ref, rows_ref, index):
    b = ids_ref[0]
    at = jnp.where(b >= 2, FROWS, 0)
    lane = jnp.full(index.shape, -1, I32)
    for k in range(FROWS):
        e = rows_ref[at + k] - BAND * b
        e = jnp.where(e < 0, jnp.where(e >= -2, e + 384, -1), jnp.where(e <= BAND + 1, e, -1))
        lane = jnp.where(index == k, e, lane)
    return lane


def pack_kernel(
    ids_ref, rows_ref, r_ref, got_first_ref, got_second_ref, tab_ref, slot_ref,
    out_ref, next_ref, hot_ref, x_ref, edge_ref, placed_ref,
):
    _, even, polar = lat_of(ids_ref)
    placed_ref[...] = placed_rows(got_first_ref, got_second_ref, edge_ref, even, polar)
    a, f, c, qc = (tab_ref[n : n + 1, :] for n in range(4))
    for i in range(0, SEG, 2):
        end = min(i + 2, SEG)
        at = slice(i, end)
        u = r_ref[0, at] + placed_ref[0, at]
        v = r_ref[1, at] + placed_ref[1, at]
        p = r_ref[3, at] + placed_ref[2, at]
        th = r_ref[4, at]
        g = v - f * u
        new_v = g - 0.25 * row_difference(p)
        new_w = r_ref[2, at] - 0.25 * level_difference(p) + 0.3 * th
        new_p = p - qc * row_difference(c * new_v) - 0.25 * level_difference(new_w)
        new_t = th - 0.3 * new_w
        for n, value in enumerate((new_v, new_w, new_p, new_t)):
            next_ref[n, at] = value
        rows = slice(LEV * i, LEV * (end + (end - i) % 2))
        for n, value in enumerate((p, g, u + f * v, new_v, new_w, new_p, new_t)):
            if (end - i) % 2:
                value = jnp.concatenate([value, jnp.zeros((1, LEV, 384), F32)], axis=0)
            high, low = split(value.reshape(-1, 384))
            x_ref[0, rows, 384 * n : 384 * n + 384] = high
            x_ref[1, rows, 384 * n : 384 * n + 384] = low
    lane = row_lanes(ids_ref, rows_ref, slot_ref[0:1, :])
    kind = slot_ref[1:2, :]
    row = iota((384, 512), 0)
    for n in range(7):
        hot_ref[384 * n : 384 * n + 384] = jnp.where(row == jnp.where(kind == n, lane, -1), 1.0, 0.0).astype(BF16)
    got = dot(x_ref[0], hot_ref[...]) + dot(x_ref[1], hot_ref[...])
    low_half = iota((8, 128), 1) < 64
    for r in range(MROWS):
        for t in range(4):
            top = got[16 * r : 16 * r + 8, 128 * t : 128 * t + 128]
            bottom = got[16 * r + 8 : 16 * r + 16, 128 * t : 128 * t + 128]
            out_ref[:, 2 * t, r, :] = jnp.where(low_half, top, shift_lanes(bottom, 64))
            out_ref[:, 2 * t + 1, r, :] = jnp.where(low_half, shift_lanes(top, 64), bottom)


def zonal_kernel(r_ref, p2_ref, from_west_ref, from_east_ref, tab_ref, out_ref, ext_ref, new_u_ref):
    a, f = tab_ref[0:1, :], tab_ref[1:2, :]
    for n, field in enumerate((0, 1, 3)):
        ext_ref[n, 2:47] = r_ref[field]
    fill_columns(ext_ref, from_west_ref, from_east_ref)
    for i, end in ((-1, 0), *CHUNKS, (45, 46)):
        new_u_ref[i + 1 : end + 1] = (
            ext_ref[0, i + 2 : end + 2]
            - (0.5 * a) * (ext_ref[2, i + 3 : end + 3] - ext_ref[2, i + 1 : end + 1])
            + f * ext_ref[1, i + 2 : end + 2]
        )
    for i, end in CHUNKS:
        out_ref[0, i:end] = new_u_ref[i + 1 : end + 1]
        out_ref[1, i:end] = p2_ref[2, i:end] - (0.5 * a) * (new_u_ref[i + 2 : end + 2] - new_u_ref[i:end])


def spectral_kernel(
    ids_ref, rows_ref, cut_ref, cos_ref, in_ref, slot_ref, fwd_ref, inv_ref, mf_ref, mi_ref, sig_ref,
    out_ref, z_ref, s_ref, y_ref, mix_ref,
):
    b, owner = ids_ref[0], ids_ref[1]
    at = jnp.where(b >= 2, FROWS, 0)
    first = 8 * (owner % 8)
    low_half = iota((96, 128), 1) < 64

    rho = slot_ref[2:3, 0:128]
    kind = slot_ref[3:4, 0:128]

    def listed(k):
        return jnp.where((k >= 0) & (k < FROWS), rows_ref[at + jnp.clip(k, 0, FROWS - 1)], -1000)

    row_at = [listed(first + t) for t in range(-4, 12)]
    cut_at = [cut_ref[at + jnp.clip(first + t, 0, FROWS - 1)] for t in range(-4, 12)]
    blank = jnp.zeros((1, 128), F32)
    rows = [jnp.full((1, 128), -1000, I32) for _ in range(5)]
    cut, c0, cp, cm = jnp.zeros((1, 128), I32), blank + 1.0, blank, blank
    for t in range(-2, 10):
        here = rho == t
        jc = jnp.clip(row_at[t + 4], 0, NLAT - 1)
        for d in range(-2, 3):
            rows[d + 2] = jnp.where(here, row_at[t + d + 4], rows[d + 2])
        cut = jnp.where(here, cut_at[t + 4], cut)
        cm = jnp.where(here, cos_ref[jc], cm)
        c0 = jnp.where(here, cos_ref[jc + 1], c0)
        cp = jnp.where(here, cos_ref[jc + 2], cp)
    j = rows[2]

    def yes(cond):
        return jnp.where(cond, 1.0, 0.0)

    up1, dn1 = yes(rows[3] == j + 1), yes(rows[1] == j - 1)
    up2, up22 = yes(rows[3] == j + 2), yes(rows[4] == j + 2)
    dn2, dn22 = yes(rows[1] == j - 2), yes(rows[0] == j - 2)
    south, north = yes(j == 0), yes(j == NLAT - 1)
    a = 0.5 * cos_ref[1] / c0
    qc = -0.25 / c0
    src, dst = iota((128, 128), 0), iota((128, 128), 1)

    def mix(n, terms):
        total = jnp.zeros((128, 128), F32)
        for to, shift, coef in terms:
            total += jnp.where(src == dst - shift, jnp.where(kind == to, coef, 0.0), 0.0)
        high, low = split(total)
        mix_ref[128 * n : 128 * n + 128, 0:128] = high
        mix_ref[128 * n : 128 * n + 128, 128:256] = low

    q0 = -0.25 * (cp * (1 - north) + cm * (1 - south) + c0 * (south + north))
    pole = 0.25 * (north - south)
    mix(0, [(2, 20, -a), (5, 24, -a)])
    mix(1, [(5, 44, -a * a)])
    mix(
        2,
        [
            (1, 10, 0.25 * up1), (1, 12, -0.25 * dn1),
            (3, 27, 0.25 * up1), (3, 29, -0.25 * dn1), (3, 17, blank - 1.0),
            (5, 44, qc * q0),
            (5, 43, qc * 0.25 * cp * up2), (5, 42, qc * 0.25 * cp * up22),
            (5, 45, qc * 0.25 * cm * dn2), (5, 46, qc * 0.25 * cm * dn22),
            (5, 32, -qc * cp * up1), (5, 34, qc * cm * dn1),
        ],
    )
    mix(
        3,
        [
            (1, 11, pole), (3, 28, pole),
            (5, 43, qc * 0.25 * (cp * yes(j == NLAT - 2) + c0 * south * up1)),
            (5, 45, qc * 0.25 * (cm * yes(j == 1) + c0 * north * dn1)),
            (5, 33, qc * c0 * (north - south)),
        ],
    )

    z_ref[:, MROWS, :] = jnp.zeros((40, 128), F32)
    z_ref[:, 24 + MROWS, :] = jnp.zeros((40, 128), F32)
    for r in range(0, MROWS, 2):
        pieces = []
        for q in range(r, min(r + 2, MROWS)):
            high, low = split(in_ref[:, q, :])
            pieces.append(jnp.concatenate([high, high, low], axis=0))
        z = dot(fwd_ref[...], pieces[0] if len(pieces) == 1 else jnp.concatenate(pieces, axis=1))
        for n in range(len(pieces)):
            z_ref[:, r + n, :] = z[0:40, 128 * n : 128 * n + 128]
            z_ref[:, 24 + r + n, :] = z[40:80, 128 * n : 128 * n + 128]

    def both_pieces(x):
        high, low = split(x)
        return jnp.concatenate(
            [jnp.concatenate([high, low], axis=1), jnp.concatenate([high, jnp.zeros_like(low)], axis=1)], axis=0
        )

    for pair in range(PAIRS):
        parts = []
        for half in range(2):
            got = dot(mf_ref[pair + PAIRS * half], both_pieces(z_ref[pair + PAIRS * half]))
            parts.append(got[:, 0:128] + got[:, 128:256])
        s_ref[pair] = jnp.where(
            low_half,
            parts[0][0:96] + shift_lanes(parts[0][96:192], 64),
            shift_lanes(parts[1][0:96], 64) + parts[1][96:192],
        )
    final = kind >= 2
    sign = jnp.where(kind == 1, -1.0, 1.0)
    k_base = 64 * (iota((96, 128), 0) % 48) + jnp.where(low_half, 0, PAIRS)
    odd_base = jnp.where(low_half, 1.0, -1.0)
    for pair in range(PAIRS):
        s = s_ref[pair]
        k = k_base + pair
        keep = jnp.minimum(k, NLON - k) <= cut
        h = jnp.where(keep, 0.0, s)
        sig = sig_ref[pair]
        d = sig * jnp.concatenate([s[48:96], s[0:48]], axis=0)
        ph = (odd_base if pair % 2 == 0 else -odd_base) * h
        high, low = split(jnp.concatenate([d, sig * sig * s, h, ph], axis=1))
        corr = dot(high, mix_ref[...])
        corr = corr[:, 0:128] + corr[:, 128:256] + dot(low, mix_ref[:, 0:128])
        s_ref[pair] = jnp.where(final, jnp.where(keep, s + corr, 0.0), sign * h + corr)
    y_ref[PAIRS:24] = jnp.zeros((24 - PAIRS, 96, 128), F32)
    for pair in range(PAIRS):
        back = dot(mi_ref[pair], both_pieces(s_ref[pair]))
        back = back[:, 0:128] + back[:, 128:256]
        y_ref[pair] = jnp.where(low_half, back[0:96], back[96:192])
    half64 = iota((64, 128), 1) < 64
    for r in range(MROWS):
        cols = []
        for i in (2 * r, 2 * r + 1):
            zz = jnp.concatenate([y_ref[:, i, :], y_ref[:, 48 + i, :]], axis=0)
            high, low = split(zz)
            cols.append(jnp.concatenate([high, high, low], axis=0))
        x = dot(inv_ref[...], jnp.concatenate(cols, axis=1))
        out_ref[:, r, :] = jnp.where(
            half64,
            x[0:64, 0:128] + shift_lanes(x[64:128, 0:128], 64),
            shift_lanes(x[0:64, 128:256], 64) + x[64:128, 128:256],
        )


def final_kernel(ids_ref, rows_ref, in_ref, next_ref, zonal_ref, tab_ref, slot_ref, hot_ref, out_ref, piece_ref, done_ref, sems):
    low_half = iota((8, 128), 1) < 64
    for r in range(MROWS):
        for t in range(4):
            even, odd = in_ref[:, 2 * t, r, :], in_ref[:, 2 * t + 1, r, :]
            top = jnp.where(low_half, even, shift_lanes(odd, 64))
            bottom = jnp.where(low_half, shift_lanes(even, 64), odd)
            high, low = split(jnp.concatenate([top, bottom], axis=0))
            piece_ref[0, 16 * r : 16 * r + 16, 128 * t : 128 * t + 128] = high
            piece_ref[1, 16 * r : 16 * r + 16, 128 * t : 128 * t + 128] = low
    rho = slot_ref[2:3, :]
    own = jnp.where((rho >= 0) & (rho < 8), 1.0, 0.0).astype(BF16)

    def spread(n):
        one_hot = hot_ref[384 * n : 384 * n + 384]
        if n < 2:
            one_hot = one_hot * own
        return (dot(piece_ref[0], one_hot, NT) + dot(piece_ref[1], one_hot, NT)).reshape(COLS, LEV, 384)

    flag = jnp.zeros((1, 384), F32)
    at = jnp.where(ids_ref[0] >= 2, FROWS, 0)
    lanes = iota((1, 384), 1)
    for k in range(FROWS):
        e = rows_ref[at + k] - BAND * ids_ref[0]
        e = jnp.where((e < 0) & (e >= -2), e + 384, e)
        flag = jnp.where(lanes == e, 1.0, flag)
    flagged = flag > 0.5
    c, qc = tab_ref[2:3, :], tab_ref[3:4, :]
    hp, dv = spread(0), spread(1)
    dv = jnp.where(flagged, dv, 0.25 * row_difference(hp))
    dp = -qc * row_difference(c * dv)

    stores = []

    def put(field, n, plain):
        done_ref[field] = jnp.where(flagged, spread(n)[0:SEG], plain)[:, :, 0:BAND]
        stores.append(pltpu.make_async_copy(done_ref.at[field], out_ref.at[field], sems.at[field]))
        stores[-1].start()

    put(1, 3, next_ref[0] + dv[0:SEG])
    put(3, 5, zonal_ref[1] + dp[0:SEG])
    put(0, 2, zonal_ref[0])
    put(2, 4, next_ref[1])
    put(4, 6, next_ref[3])
    for store in stores:
        store.wait()


VMEM = pl.BlockSpec(memory_space=pltpu.VMEM)
SMEM = pl.BlockSpec(memory_space=pltpu.SMEM)
ANY = pl.BlockSpec(memory_space=pl.ANY)


def call(body, name, specs, args, outs, scratch, flops, mib, out_spec=None):
    return pl.pallas_call(
        body,
        name=name,
        out_shape=outs,
        in_specs=list(specs),
        out_specs=jax.tree.map(lambda _: out_spec or VMEM, outs),
        scratch_shapes=scratch,
        compiler_params=pltpu.CompilerParams(vmem_limit_bytes=mib << 20),
        cost_estimate=pl.CostEstimate(flops=flops, bytes_accessed=8 << 20, transcendentals=0),
    )(*args)


def shape(*dims):
    return jax.ShapeDtypeStruct(dims, F32)


def neighbours():
    first, second = [], []
    for l in range(64):
        for b in (0, 2):
            first += [(64 * b + l, 64 * b + 64 + l), (64 * b + 64 + l, 64 * b + l)]
        second += [(64 + l, 128 + l), (128 + l, 64 + l)]
        second += [(l, (l + 32) % 64), (192 + l, 192 + (l + 32) % 64)]
    return first, second


def exchange(edges):
    east, west, first, second = edges
    pairs_first, pairs_second = neighbours()
    got_first = lax.ppermute(first, ("lat", "lon"), pairs_first)
    got_second = lax.ppermute(second, ("lat", "lon"), pairs_second)
    from_west = lax.ppermute(east, "lon", [(i, (i + 1) % 64) for i in range(64)])
    from_east = lax.ppermute(west, "lon", [((i + 1) % 64, i) for i in range(64)])
    return from_west, from_east, got_first, got_second


def row_tables(b):
    def cosine(row):
        return jnp.abs(jnp.sin((row.astype(F32) + 0.5) * (jnp.pi / NLAT)))

    lane = jnp.arange(384, dtype=I32)
    row = jnp.where(lane < 370, lane, lane - 384) + BAND * b
    c = cosine(row)
    f = -0.2 * jnp.cos((row.astype(F32) + 0.5) * (jnp.pi / NLAT))
    polar = cosine(jnp.zeros((), I32))
    zero = jnp.zeros_like(c)
    tab = jnp.stack([0.5 * polar / c, f, c, 0.25 / c, zero, zero, zero, zero])
    return tab, cosine(jnp.arange(-1, 1447, dtype=I32))


def per_device(prognostic, filter_rows, cutoff):
    b, lon = lax.axis_index("lat"), lax.axis_index("lon")
    ids = jnp.stack([b, lon]).astype(I32)
    tab, cosines = row_tables(b)
    tab, cosines = lax.optimization_barrier((tab, cosines))
    rho64, kind64 = slot_tables()
    slots = np.full((8, 512), -1, np.int32)
    slots[0] = (8 * np.arange(8)[:, None] + rho64[None, :]).reshape(-1)
    slots[1] = np.tile(kind64, 8)
    slots[2] = np.tile(rho64, 8)
    slots[3] = np.tile(kind64, 8)
    margin = (slots[2] < 0) | (slots[2] > 7)
    slots[3] = np.where(margin & (slots[1] == 1), 0, slots[3])
    slots = jnp.asarray(slots)
    constants = [jnp.asarray(x) for x in fourier_constants()]

    start = prognostic.transpose(0, 2, 1, 3)
    edge_shapes = (shape(4, 8, 384), shape(4, 8, 384), shape(2, EDGE), shape(2, EDGE))
    edges = call(
        edges_kernel, "edges", (SMEM, VMEM), (ids, start), edge_shapes,
        [pltpu.VMEM((3, SEG, LEV, 384), F32)], 10**7, 16,
    )
    state, *edges = call(
        first_kernel, "first", (SMEM, *[VMEM] * 6), (ids, start, *exchange(edges), tab),
        (shape(5, SEG, LEV, 384), *edge_shapes),
        [pltpu.VMEM((3, 49, LEV, 384), F32), pltpu.VMEM((16, EDGE), F32), pltpu.VMEM((47, LEV, 384), F32)],
        10**8, 24,
    )
    from_west, from_east, got_first, got_second = exchange(edges)
    message, after, hot = call(
        pack_kernel, "pack", (SMEM, SMEM, *[VMEM] * 5),
        (ids, filter_rows, state, got_first, got_second, tab, slots),
        (shape(8, 8, MROWS, 128), shape(4, SEG, LEV, 384), jax.ShapeDtypeStruct((7 * 384, 512), BF16)),
        [
            pltpu.VMEM((2, LEV * COLS, 7 * 384), BF16),
            pltpu.VMEM((16, EDGE), F32),
            pltpu.VMEM((3, SEG, LEV, 384), F32),
        ],
        10**9, 32,
    )
    zonal = call(
        zonal_kernel, "zonal", [VMEM] * 5, (state, after, from_west, from_east, tab),
        shape(2, SEG, LEV, 384),
        [pltpu.VMEM((3, 49, LEV, 384), F32), pltpu.VMEM((47, LEV, 384), F32)], 10**8, 16,
    )
    message, zonal = lax.optimization_barrier((message, zonal))
    whole = lax.all_to_all(message.reshape(64, MROWS, 128), "lon", split_axis=0, concat_axis=0, tiled=True)
    answer = call(
        spectral_kernel, "spectral", (*[SMEM] * 4, *[VMEM] * 7),
        (ids, filter_rows, cutoff, cosines, whole, slots, *constants),
        shape(64, MROWS, 128),
        [
            pltpu.VMEM((40, 48, 128), F32),
            pltpu.VMEM((PAIRS, 96, 128), F32),
            pltpu.VMEM((24, 96, 128), F32),
            pltpu.VMEM((512, 256), BF16),
        ],
        10**9, 32,
    )
    back = lax.all_to_all(answer, "lon", split_axis=0, concat_axis=0, tiled=True)
    out = call(
        final_kernel, "final", (SMEM, SMEM, *[VMEM] * 6),
        (ids, filter_rows, back.reshape(8, 8, MROWS, 128), after, zonal, tab, slots, hot),
        shape(FIELDS, SEG, LEV, BAND),
        [
            pltpu.VMEM((2, LEV * COLS, 512), BF16),
            pltpu.VMEM((FIELDS, SEG, LEV, BAND), F32),
            pltpu.SemaphoreType.DMA((FIELDS,)),
        ],
        10**9, 32, ANY,
    )
    return out.transpose(0, 2, 1, 3)


def solution(mesh):
    in_specs = (P(None, None, "lon", "lat"), P(), P())
    out_specs = P(None, None, "lon", "lat")
    return jax.shard_map(
        per_device, mesh=mesh, in_specs=in_specs, out_specs=out_specs, check_vma=False
    )
```
